32 devices in a mesh: img: 4 (over y, core), txt: 8 (over z, x).
Axes of the slice: x: 2, y: 2, z: 4, core: 2. Of those that a mesh axis runs over, the one named last changes fastest.
Arguments:
- picture_feature_vectors: bfloat16 [4096, 256], P(('img', 'txt')), may hold values from -400 to 400
- wording_feature_vectors: bfloat16 [4096, 256], P('txt'), may hold values from -400 to 400
- logit_softness: float32 [1], replicated, may hold values from 0.0025 to 0.1
- attention_request_vectors: bfloat16 [64, 35, 768], P(('img', 'txt')), may hold values from -64 to 64
- attention_lookup_vectors: bfloat16 [64, 257, 768], P(('img', 'txt')), may hold values from -32 to 32
- attention_content_vectors: bfloat16 [64, 257, 768], P(('img', 'txt')), may hold values from -6 to 6
- picture_distractor_partition: int32 [64, 4], P('img'), may hold values from 0 to 7, all different within a row; in each aligned block of 2 rows (0 to 1, 2 to 3, ...) at most 2 rows name the same one
- picture_distractor_slot: int32 [64, 4], P('img'), may hold values from 0 to 1
- wording_distractor_partition: int32 [64, 4], P('img'), may hold values from 0 to 7, all different within a row; in each aligned block of 2 rows (0 to 1, 2 to 3, ...) at most 2 rows name the same one
- wording_distractor_slot: int32 [64, 4], P('img'), may hold values from 0 to 1
- picture_couple_adjoint: bfloat16 [64, 4, 35, 768], P(('img', 'txt')), may hold values from -6 to 6
- wording_couple_adjoint: bfloat16 [64, 4, 35, 768], P(('img', 'txt')), may hold values from -6 to 6
Outputs:
- image_loss: float32 [4096], P(('img', 'txt'))
- text_loss: float32 [4096], P('txt')
- img_pair_out: bfloat16 [64, 4, 35, 768], P(('img', 'txt'))
- txt_pair_out: bfloat16 [64, 4, 35, 768], P(('img', 'txt'))
- query_grad: bfloat16 [64, 35, 768], P(('img', 'txt'))
- key_grad: bfloat16 [64, 257, 768], P(('img', 'txt'))
- value_grad: bfloat16 [64, 257, 768], P(('img', 'txt'))
The draws below stay inside these ranges and needn't reach their ends.
Inputs may be any that keep to these rules, and one draw needn't show every extreme that they name: `picture_distractor_partition`: each row names 4 different shards. Among the rows of one device (aligned blocks of 2 rows) no shard is named more than 2 times, and in some such block a shard is named exactly 2 times. `wording_distractor_partition`: each row names 4 different shards. Among the rows of one device (aligned blocks of 2 rows) no shard is named more than 2 times, and in some such block a shard is named exactly 2 times.
All inputs are finite; a program needn't handle non-finite values.
Results may differ from the reference program's by a relative error of at most 0.0059.
Values may be sent and summed in bfloat16 or wider, within the bound.
No kernel may reach another device: no remote copies, remote signals or barrier semaphores. Data moves between devices by JAX's collectives and lax.ppermute only.
A program may use at most 256 MiB of HBM per device.

```python
import math
import jax
import jax.numpy as jnp
import numpy as np
from jax import lax

EMB = 256
HEADS = 12
PATCHES = 257
CAPTION = 35
NEGS = 4
UNITE_DEV = 2
WIDTH = 768
PAIRS = 4096
UNITED = 64
MOST = 2
N_TXT = 8


def shared_rows(key):
    first_key = jax.random.fold_in(key, 0)
    base_rows = jnp.clip(jax.random.normal(first_key, (PAIRS, EMB), jnp.float32), -4.0, 4.0)
    return base_rows


def draw_picture_feature_vectors(key, part):
    base_rows = shared_rows(key)
    key = jax.random.fold_in(key, 3)
    first_key = jax.random.fold_in(key, 0)
    return (0.5 * base_rows + jnp.clip(jax.random.normal(first_key, (PAIRS, EMB), jnp.float32), -4.0, 4.0)).astype(jnp.bfloat16)


def draw_wording_feature_vectors(key, part):
    base_rows = shared_rows(key)
    key = jax.random.fold_in(key, 5)
    first_key = jax.random.fold_in(key, 0)
    return (0.5 * base_rows + jnp.clip(jax.random.normal(first_key, (PAIRS, EMB), jnp.float32), -4.0, 4.0)).astype(jnp.bfloat16)


def draw_logit_softness(key, part):
    key = jax.random.fold_in(key, 7)
    return jax.random.uniform(key, (1,), jnp.float32, 0.05, 0.1)


def draw_attention_request_vectors(key, part):
    key = jax.random.fold_in(key, 9)
    first_key = jax.random.fold_in(key, 0)
    return jnp.clip(2.0 * jax.random.normal(first_key, (UNITED, CAPTION, WIDTH), jnp.float32), -8.0, 8.0).astype(jnp.bfloat16)


def draw_attention_lookup_vectors(key, part):
    key = jax.random.fold_in(key, 13)
    first_key = jax.random.fold_in(key, 0)
    return jnp.clip(jax.random.normal(first_key, (UNITED, PATCHES, WIDTH), jnp.float32), -6.0, 6.0).astype(jnp.bfloat16)


def with_ends(values, rng, least, high):
    place = [jax.random.randint(jax.random.fold_in(rng, axis), (), 0, length) for axis, length in enumerate(values.shape)]
    widest = values.shape.index(max(values.shape))
    beside = place[:widest] + [(place[widest] + 1) % values.shape[widest]] + place[widest + 1:]
    return values.at[tuple(place)].set(least).at[tuple(beside)].set(high)


def block_scale(own_key, dims, cuts, smallest, largest):
    factor_of, own = 1.0, jax.random.fold_in(own_key, 6)
    for dim, shards_of in cuts:
        steps = jnp.exp(jax.random.uniform(jax.random.fold_in(own, dim), (shards_of,), jnp.float32, smallest / len(cuts), largest / len(cuts)))
        factor_of = factor_of * jnp.repeat(steps, dims[dim] // shards_of).reshape([-1 if axis == dim else 1 for axis in range(len(dims))])
    return factor_of


def routed_block(key, own, number, rows, amount, top, reach, slope):
    order = jax.random.permutation(key, amount)
    crowded, ordinary = load_shares(amount, rows * top, reach, slope, True), load_shares(amount, rows * top, reach, slope, False)
    places = jnp.arange(amount)

    def named(sizes, turn):
        used = int((sizes > 0).sum())
        fixed = max(1, used // 4)
        moved = fixed + (places - fixed + turn * (used - fixed)) % max(1, amount - fixed)
        return jnp.zeros((amount,), jnp.int32).at[order[jnp.where(places < fixed, places, moved)]].set(jnp.asarray(sizes, jnp.int32))

    sizes = jnp.where(number % 4 == 0, named(crowded, number // 4), named(ordinary, number - number // 4 - 1))
    mixed = jax.random.permutation(jax.random.fold_in(own, 3), amount)
    giver, sink = mixed[0:amount // 2 * 2:2], mixed[1:amount // 2 * 2:2]
    margin = jnp.minimum(sizes[giver] - 1, reach - sizes[sink]) // 2
    margin = jnp.where((giver == order[0]) | (sink == order[0]) | (sizes[sink] == 0), 0, jnp.maximum(margin, 0))
    moved = jax.random.randint(jax.random.fold_in(own, 4), (amount // 2,), 0, 1 << 20) % (margin + 1)
    sizes = sizes.at[giver].add(-moved).at[sink].add(moved)
    members = jnp.searchsorted(jnp.cumsum(sizes), jnp.arange(rows * top), side="right").astype(jnp.int32)
    table = members.reshape(top, rows).T
    table = table[jax.random.permutation(jax.random.fold_in(own, 1), rows)]
    turn = jax.random.randint(jax.random.fold_in(own, 2), (rows, 1), 0, top)
    return jnp.take_along_axis(table, (jnp.arange(top)[None, :] + turn) % top, axis=1)


def load_shares(amount, total, bound, slope, full):
    portions = [(1 << 20) // math.isqrt(rank ** slope) + 1 for rank in range(1, amount + 1)]
    largest = bound if full else min(bound, max(-(-total // amount), total * portions[0] // sum(portions)))
    least = 1 if total - largest >= amount - 1 else 0
    given, surplus = [largest] + [least] * (amount - 1), total - largest - least * (amount - 1)
    while surplus > 0:
        movable = [i for i in range(1, amount) if given[i] < largest] or [i for i in range(1, amount) if given[i] < bound]
        mass, budget = sum([portions[i] for i in movable]), surplus
        for i in movable:
            more = min(bound - given[i], max(1, budget * portions[i] // mass), surplus)
            given[i] = given[i] + more
            surplus = surplus - more
    return np.array(given)


def noise(rng, extent, scale, limit, cuts=(), held_as=jnp.bfloat16):
    result = jax.random.normal(rng, extent, jnp.float32) * scale
    if len(cuts) > 0:
        result = block_scale(rng, extent, cuts, -0.22, 0.18) * result
    return jnp.clip(result, min=-limit, max=limit).astype(held_as)


def setup_inputs(seed: int = 0) -> dict:
    keys = jax.random.split(jax.random.key(seed), 13)
    picture_feature_vectors = draw_picture_feature_vectors(jax.random.fold_in(keys[12], 71), 0)
    wording_feature_vectors = draw_wording_feature_vectors(jax.random.fold_in(keys[12], 71), 0)
    logit_softness = draw_logit_softness(jax.random.fold_in(keys[12], 71), 0)
    attention_request_vectors = draw_attention_request_vectors(jax.random.fold_in(keys[12], 71), 0)
    attention_lookup_vectors = draw_attention_lookup_vectors(jax.random.fold_in(keys[12], 71), 0)
    attention_content_vectors = noise(keys[5], (UNITED, PATCHES, WIDTH), 1.0, 6.0, ((0, 32),))
    picture_distractor_partition_keys = jax.random.split(jax.random.fold_in(keys[6], 1), UNITED // UNITE_DEV)
    picture_distractor_partition_turns = jax.random.permutation(jax.random.fold_in(keys[6], 3), UNITED // UNITE_DEV)
    picture_distractor_partition = jax.vmap(lambda own, number: routed_block(jax.random.fold_in(keys[6], 2), own, number, UNITE_DEV, N_TXT, NEGS, MOST, 2))(picture_distractor_partition_keys, picture_distractor_partition_turns).reshape((UNITED, NEGS))
    picture_distractor_slot = with_ends(jax.random.randint(keys[7], (UNITED, NEGS), 0, UNITE_DEV), jax.random.fold_in(keys[7], 1), 0, UNITE_DEV - 1).astype(jnp.int32)
    wording_distractor_partition_keys = jax.random.split(jax.random.fold_in(keys[8], 1), UNITED // UNITE_DEV)
    wording_distractor_partition_turns = jax.random.permutation(jax.random.fold_in(keys[8], 3), UNITED // UNITE_DEV)
    wording_distractor_partition = jax.vmap(lambda own, number: routed_block(jax.random.fold_in(keys[8], 2), own, number, UNITE_DEV, N_TXT, NEGS, MOST, 2))(wording_distractor_partition_keys, wording_distractor_partition_turns).reshape((UNITED, NEGS))
    wording_distractor_slot = with_ends(jax.random.randint(keys[9], (UNITED, NEGS), 0, UNITE_DEV), jax.random.fold_in(keys[9], 1), 0, UNITE_DEV - 1).astype(jnp.int32)
    picture_couple_adjoint = noise(keys[10], (UNITED, NEGS, CAPTION, WIDTH), 1.0, 6.0, ((0, 32),))
    wording_couple_adjoint = noise(keys[11], (UNITED, NEGS, CAPTION, WIDTH), 1.0, 6.0, ((0, 32),))
    return dict(picture_feature_vectors=picture_feature_vectors, wording_feature_vectors=wording_feature_vectors, logit_softness=logit_softness, attention_request_vectors=attention_request_vectors, attention_lookup_vectors=attention_lookup_vectors, attention_content_vectors=attention_content_vectors, picture_distractor_partition=picture_distractor_partition, picture_distractor_slot=picture_distractor_slot, wording_distractor_partition=wording_distractor_partition, wording_distractor_slot=wording_distractor_slot, picture_couple_adjoint=picture_couple_adjoint, wording_couple_adjoint=wording_couple_adjoint)


EPSILON = 1e-06

def normalize_rows(projection):
    widened = projection.astype(jnp.float32)
    factor = lax.rsqrt(lax.optimization_barrier(jnp.sum(widened * widened, axis=-1, keepdims=True)) + EPSILON)
    return (widened * factor).astype(jnp.bfloat16)

def attend_forward(query_part, key_part, value_part, factor):
    logits = jnp.einsum('bqhd,bphd->bhqp', query_part.astype(jnp.float32), key_part.astype(jnp.float32)) * factor
    shifted = jnp.exp(logits - lax.optimization_barrier(jnp.max(logits, axis=-1, keepdims=True)))
    weights = shifted / lax.optimization_barrier(jnp.sum(shifted, axis=-1, keepdims=True))
    rounded = weights.astype(jnp.bfloat16)
    output = jnp.einsum('bhqp,bphd->bqhd', rounded.astype(jnp.float32), value_part.astype(jnp.float32))
    return (weights, rounded, output)

def attend_backward(query_part, key_part, value_part, weights, rounded, upstream, factor):
    upstream_wide = upstream.astype(jnp.float32)
    value_term = jnp.einsum('bhqp,bqhd->bphd', rounded.astype(jnp.float32), upstream_wide)
    weight_term = jnp.einsum('bqhd,bphd->bhqp', upstream_wide, value_part.astype(jnp.float32))
    inner_sum = lax.optimization_barrier(jnp.sum(weights * weight_term, axis=-1, keepdims=True))
    logit_term = (weights * (weight_term - inner_sum) * factor).astype(jnp.bfloat16)
    query_term = jnp.einsum('bhqp,bphd->bqhd', logit_term.astype(jnp.float32), key_part.astype(jnp.float32))
    key_term = jnp.einsum('bhqp,bqhd->bphd', logit_term.astype(jnp.float32), query_part.astype(jnp.float32))
    return (query_term, key_term, value_term)

def reference(picture_feature_vectors, wording_feature_vectors, logit_softness, attention_request_vectors, attention_lookup_vectors, attention_content_vectors, picture_distractor_partition, picture_distractor_slot, wording_distractor_partition, wording_distractor_slot, picture_couple_adjoint, wording_couple_adjoint):
    reordering_undo = 1.0 / logit_softness[0]
    unit_images = normalize_rows(picture_feature_vectors)
    unit_texts = normalize_rows(wording_feature_vectors)
    pair_count = unit_images.shape[0]
    block_rows = math.gcd(pair_count, 1024)
    diagonal = lax.optimization_barrier(jnp.sum(unit_images.astype(jnp.float32) * unit_texts.astype(jnp.float32), axis=1)) * reordering_undo

    def image_lse(row_block):
        logits = jnp.dot(row_block, unit_texts.T, preferred_element_type=jnp.float32) * reordering_undo
        highest = lax.optimization_barrier(jnp.max(logits, axis=1))
        return highest + jnp.log(lax.optimization_barrier(jnp.sum(jnp.exp(logits - highest[:, None]), axis=1)))

    def text_lse(row_block):
        logits = jnp.dot(row_block, unit_images.T, preferred_element_type=jnp.float32) * reordering_undo
        highest = lax.optimization_barrier(jnp.max(logits, axis=1))
        return highest + jnp.log(lax.optimization_barrier(jnp.sum(jnp.exp(logits - highest[:, None]), axis=1)))
    image_loss = lax.map(image_lse, unit_images.reshape(-1, block_rows, EMB)).reshape(-1) - diagonal
    text_loss = lax.map(text_lse, unit_texts.reshape(-1, block_rows, EMB)).reshape(-1) - diagonal
    united = attention_request_vectors.shape[0]
    caption = attention_request_vectors.shape[1]
    width = attention_request_vectors.shape[2]
    patches = attention_lookup_vectors.shape[1]
    head_dim = width // HEADS
    factor = 1.0 / math.sqrt(head_dim)
    group_size = UNITE_DEV * N_TXT
    group_base = jnp.arange(united, dtype=jnp.int32) // group_size * group_size
    image_texts = (group_base[:, None] + picture_distractor_partition * UNITE_DEV + picture_distractor_slot).astype(jnp.int32)
    text_images = (group_base[:, None] + wording_distractor_partition * UNITE_DEV + wording_distractor_slot).astype(jnp.int32)
    query_heads = attention_request_vectors.reshape(united, caption, HEADS, head_dim)
    key_heads = attention_lookup_vectors.reshape(united, patches, HEADS, head_dim)
    value_heads = attention_content_vectors.reshape(united, patches, HEADS, head_dim)

    def image_side(inputs):
        picks, key_one, value_one, upstream = inputs
        query_part = query_heads[picks].reshape(1, NEGS * caption, HEADS, head_dim)
        key_part = key_one[None]
        value_part = value_one[None]
        weights, rounded, output = attend_forward(query_part, key_part, value_part, factor)
        query_term, key_term, value_term = attend_backward(query_part, key_part, value_part, weights, rounded, upstream.reshape(1, NEGS * caption, HEADS, head_dim), factor)
        return (output.reshape(NEGS, caption, width).astype(jnp.bfloat16), query_term.reshape(NEGS, caption, width).astype(jnp.bfloat16), key_term.reshape(patches, width), value_term.reshape(patches, width))
    img_pair_out, image_qterms, key_start, value_start = lax.map(image_side, (image_texts, key_heads, value_heads, picture_couple_adjoint))

    def text_side(totals, inputs):
        key_acc, value_acc = totals
        picks, query_one, upstream = inputs
        query_part = jnp.broadcast_to(query_one[None], (NEGS, caption, HEADS, head_dim))
        key_part = key_heads[picks]
        value_part = value_heads[picks]
        weights, rounded, output = attend_forward(query_part, key_part, value_part, factor)
        query_term, key_term, value_term = attend_backward(query_part, key_part, value_part, weights, rounded, upstream.reshape(NEGS, caption, HEADS, head_dim), factor)
        key_acc = key_acc.at[picks].add(key_term.reshape(NEGS, patches, width))
        value_acc = value_acc.at[picks].add(value_term.reshape(NEGS, patches, width))
        narrow_terms = lax.optimization_barrier(query_term.astype(jnp.bfloat16))
        query_sum = lax.optimization_barrier(jnp.sum(narrow_terms.astype(jnp.float32), axis=0)).reshape(caption, width)
        return ((key_acc, value_acc), (output.reshape(NEGS, caption, width).astype(jnp.bfloat16), query_sum))
    (key_total, value_total), (txt_pair_out, text_qsum) = lax.scan(text_side, (key_start, value_start), (text_images, query_heads, wording_couple_adjoint))
    query_total = text_qsum + jnp.zeros((united, caption, width), jnp.float32).at[image_texts.reshape(-1)].add(image_qterms.reshape(-1, caption, width).astype(jnp.float32))
    return (image_loss, text_loss, img_pair_out, txt_pair_out, query_total.astype(jnp.bfloat16), key_total.astype(jnp.bfloat16), value_total.astype(jnp.bfloat16))
```

```python
import functools
import math

import jax
import jax.numpy as jnp
from jax import lax
from jax.experimental import pallas as pl
from jax.experimental.pallas import tpu as pltpu
from jax.sharding import PartitionSpec as P

HEADS = 12
NEGS = 4
EPSILON = 1e-06
LANES = 128
VMEM = pl.BlockSpec(memory_space=pltpu.VMEM)
SMEM = pl.BlockSpec(memory_space=pltpu.SMEM)
F32 = jnp.float32
BF16 = jnp.bfloat16
NT = (((1,), (1,)), ((), ()))
NN = (((1,), (0,)), ((), ()))


def kernel_call(body, out_shape, n_smem, n_vmem, scratch=(), flops=0, nbytes=0):
    return pl.pallas_call(
        body,
        out_shape=out_shape,
        in_specs=[SMEM] * n_smem + [VMEM] * n_vmem,
        out_specs=jax.tree.map(lambda _: VMEM, out_shape),
        scratch_shapes=list(scratch),
        compiler_params=pltpu.CompilerParams(vmem_limit_bytes=40 * 1024 * 1024),
        cost_estimate=pl.CostEstimate(flops=flops, bytes_accessed=nbytes, transcendentals=0),
    )


def dot(a, b, dims):
    return lax.dot_general(a, b, dims, preferred_element_type=F32)


def send_body(owners, place, cots, sent):
    rows = cots.shape[0]
    sent[...] = jnp.zeros_like(sent)
    for row in range(rows):
        for entry in range(NEGS):
            sent[owners[place[0] * rows + row, entry], row] = cots[row, entry]


def contrast_body(place, softness, images, texts, row_stats, col_stats, unit_images, unit_texts):
    for source, unit in ((images, unit_images), (texts, unit_texts)):
        wide = source[...].astype(F32)
        factor = lax.rsqrt(jnp.sum(wide * wide, axis=-1, keepdims=True) + EPSILON)
        unit[...] = (wide * factor).astype(BF16)
    undo = 1.0 / softness[0]
    n_images, n_texts = images.shape[0], texts.shape[0]
    first_image, first_text = place[1] * n_images, place[0] * n_texts

    def stats(long, long_first, short, short_first):
        logits = dot(long, short, NT) * undo
        highest = jnp.max(logits, axis=0, keepdims=True)
        total = jnp.sum(jnp.exp(logits - highest), axis=0, keepdims=True)
        on_diag = (lax.broadcasted_iota(jnp.int32, logits.shape, 0) + long_first) == (
            lax.broadcasted_iota(jnp.int32, logits.shape, 1) + short_first
        )
        diag = jnp.sum(jnp.where(on_diag, logits, 0.0), axis=0, keepdims=True)
        return highest + jnp.log(total), diag

    for block in range(n_images // LANES):
        first = block * LANES
        lse, diag = stats(
            unit_texts[...], first_text, unit_images[first : first + LANES, :], first_image + first
        )
        row_stats[block, 0:1, :] = lse
        row_stats[block, 1:2, :] = diag
    for block in range(n_texts // LANES):
        first = block * LANES
        lse, diag = stats(
            unit_images[...], first_image, unit_texts[first : first + LANES, :], first_text + first
        )
        col_stats[0:1, first : first + LANES] = lse
        col_stats[1:2, first : first + LANES] = diag


def attend(image, q_at, g_at, queries, cots, keys, values, key_sum, value_sum, key_last, value_last, emit):
    rows = queries.shape[1]
    stack = rows * NEGS
    patches = keys.shape[1] - 1
    half = LANES // 2

    def tile_step(tile, _):
        lanes = pl.ds(pl.multiple_of(tile * LANES, LANES), LANES)
        low = lax.broadcasted_iota(jnp.int32, (stack, LANES), 1) < half
        q = jnp.concatenate([queries[at, :, lanes] for at in q_at], axis=0)
        g = jnp.concatenate([cots[at, :, lanes] for at in g_at], axis=0)
        q2 = jnp.concatenate([jnp.where(low, q, 0.0), jnp.where(low, 0.0, q)], axis=0)
        g2 = jnp.concatenate([jnp.where(low, g, 0.0), jnp.where(low, 0.0, g)], axis=0)
        key, value = keys[image, 0:patches, lanes], values[image, 0:patches, lanes]
        key_end = keys[image, patches : patches + 1, lanes].astype(F32)
        value_end = values[image, patches : patches + 1, lanes].astype(F32)
        logits = dot(q2.astype(BF16), key, NT)
        logit_end = jnp.sum(q2 * key_end, axis=-1, keepdims=True)
        highest = jnp.maximum(jnp.max(logits, axis=-1, keepdims=True), logit_end)
        shifted = jnp.exp(logits - highest)
        shifted_end = jnp.exp(logit_end - highest)
        inverse = 1.0 / (jnp.sum(shifted, axis=-1, keepdims=True) + shifted_end)
        weights = shifted * inverse
        weight_end = shifted_end * inverse
        rounded = weights.astype(BF16)
        rounded_end = weight_end.astype(BF16).astype(F32)
        output = dot(rounded, value, NN) + rounded_end * value_end
        term = dot(g2.astype(BF16), value, NT)
        term_end = jnp.sum(g2 * value_end, axis=-1, keepdims=True)
        inner = jnp.sum(weights * term, axis=-1, keepdims=True) + weight_end * term_end
        logit_term = (weights * (term - inner)).astype(BF16)
        logit_term_end = (weight_end * (term_end - inner)).astype(BF16).astype(F32)
        q_term = (dot(logit_term, key, NN) + logit_term_end * key_end) * 0.125
        emit(
            lanes,
            jnp.where(low, output[:stack], output[stack:]),
            jnp.where(low, q_term[:stack], q_term[stack:]),
        )
        q_turned = jnp.transpose(q).astype(BF16)
        g_turned = jnp.transpose(g).astype(BF16)
        for head in range(2):
            at = pl.ds(pl.multiple_of(tile * LANES, LANES) + head * half, half)
            part = slice(head * half, head * half + half)
            line = slice(head * stack, head * stack + stack)
            key_sum[image, at, :] += dot(q_turned[part], logit_term[line], NN)
            value_sum[image, at, :] += dot(g_turned[part], rounded[line], NN)
        key_last[image, :, lanes] += jnp.sum(logit_term_end * q2, axis=0, keepdims=True)
        value_last[image, :, lanes] += jnp.sum(rounded_end * g2, axis=0, keepdims=True)
        return 0

    lax.fori_loop(0, keys.shape[2] // LANES, tile_step, 0)


def widen(source, wide, at, scale=1.0):
    caption = source.shape[0]
    wide[at, caption:, :] = jnp.zeros((wide.shape[1] - caption, wide.shape[2]), F32)
    wide[at, 0:caption, :] = source.astype(F32) * scale


def image_body(n_parts, owners, slots, place, *refs):
    parts, refs = refs[:n_parts], refs[n_parts:]
    cots, keys, values, out, key_sum, value_sum, key_last, value_last, q_sum, queries, wide = refs
    images, captions = keys.shape[0], parts[0].shape[0]
    caption = parts[0].shape[1]
    for part in range(n_parts):
        for row in range(captions):
            widen(parts[part][row], queries, part * captions + row, 0.125)
    for image in range(images):
        for entry in range(NEGS):
            widen(cots[image, entry], wide, image * NEGS + entry)
    for total in (key_sum, value_sum, key_last, value_last, q_sum):
        total[...] = jnp.zeros_like(total)

    def image_step(image, _):
        line = place[0] * images + image
        at = [
            jnp.bitwise_xor(owners[line, e], place[0]) * captions + slots[line, e] for e in range(NEGS)
        ]
        rows = queries.shape[1]

        def emit(lanes, output, q_term):
            for e in range(NEGS):
                out[image, e, :, lanes] = output[e * rows : e * rows + caption].astype(BF16)
                q_sum[at[e], :, lanes] += (
                    q_term[e * rows : (e + 1) * rows].astype(BF16).astype(F32)
                )

        attend(
            image, at, [image * NEGS + e for e in range(NEGS)], queries, wide, keys, values,
            key_sum, value_sum, key_last, value_last, emit,
        )
        return 0

    lax.fori_loop(0, images, image_step, 0)


def text_body(n_parts, owners, slots, place, *refs):
    parts, refs = refs[:n_parts], refs[n_parts:]
    (cots, keys, values, key_in, value_in, key_last_in, value_last_in, q_in,
     out, q_out, key_grad, value_grad,
     queries, wide, outs, key_sum, value_sum, key_last, value_last, q_sum, lists, counts) = refs
    images, captions = keys.shape[0], parts[0].shape[0]
    caption = parts[0].shape[1]
    rows = queries.shape[1]
    patches = keys.shape[1] - 1
    everyone = n_parts * captions
    for part in range(n_parts):
        for row in range(captions):
            widen(parts[part][row], queries, part * captions + row, 0.125)
            widen(cots[part, row], wide, part * captions + row)
    for ref in (queries, wide):
        ref[everyone] = jnp.zeros(ref.shape[1:], F32)
    key_sum[...] = key_in[...]
    value_sum[...] = value_in[...]
    key_last[...] = key_last_in[...]
    value_last[...] = value_last_in[...]
    q_sum[0:everyone] = q_in[...]
    outs[...] = jnp.zeros_like(outs)
    for image in range(images):
        counts[image] = 0

        def clear(i, _, image=image):
            lists[image, i] = everyone
            return 0

        lax.fori_loop(0, lists.shape[1], clear, 0)

    def find(j, _):
        for entry in range(NEGS):

            @pl.when(owners[j, entry] == place[0])
            def _():
                image = slots[j, entry]
                lists[image, counts[image]] = j
                counts[image] = counts[image] + 1

        return 0

    lax.fori_loop(0, everyone, find, 0)

    def image_step(image, _):
        def chunk_step(chunk, _):
            j = [lists[image, chunk * NEGS + e] for e in range(NEGS)]
            q_at = [
                jnp.where(
                    j[e] < everyone,
                    jnp.bitwise_xor(j[e] // captions, place[0]) * captions + j[e] % captions,
                    everyone,
                )
                for e in range(NEGS)
            ]

            def emit(lanes, output, q_term):
                for e in range(NEGS):
                    outs[j[e], :, lanes] = output[e * rows : (e + 1) * rows]
                    q_sum[q_at[e], :, lanes] += (
                        q_term[e * rows : (e + 1) * rows].astype(BF16).astype(F32)
                    )

            attend(
                image, q_at, j, queries, wide, keys, values,
                key_sum, value_sum, key_last, value_last, emit,
            )
            return 0

        lax.fori_loop(0, (counts[image] + NEGS - 1) // NEGS, chunk_step, 0)
        return 0

    lax.fori_loop(0, images, image_step, 0)

    def finish(part, _):
        source = jnp.bitwise_xor(part, place[0])
        for row in range(captions):
            out[part, row] = outs[part * captions + row, 0:caption, :].astype(BF16)
            q_out[part, row] = q_sum[source * captions + row, 0:caption, :].astype(BF16)
        return 0

    lax.fori_loop(0, n_parts, finish, 0)
    for total, last, grad in ((key_sum, key_last, key_grad), (value_sum, value_last, value_grad)):
        for image in range(images):
            for tile in range(keys.shape[2] // LANES):
                lanes = slice(tile * LANES, (tile + 1) * LANES)
                grad[image, 0:patches, lanes] = jnp.transpose(total[image, lanes, :]).astype(BF16)
            grad[image, patches : patches + 1, :] = last[image].astype(BF16)


def join_body(owners, place, got_out, got_q, pair_out, q_grad):
    rows = pair_out.shape[0]
    for row in range(rows):
        for entry in range(NEGS):
            pair_out[row, entry] = got_out[owners[place[0] * rows + row, entry], row]
        total = got_q[0, row].astype(F32)
        for source in range(1, got_q.shape[0]):
            total = total + got_q[source, row].astype(F32)
        q_grad[row] = total.astype(BF16)


def gathered(block, axis):
    size = lax.axis_size(axis)
    half = size // 2

    def swap(part, mask):
        return lax.ppermute(part, axis, [(s, s ^ mask) for s in range(size)])

    other = swap(block, half)
    near = [block] + [swap(block, mask) for mask in range(1, half)]
    far = [other] + [swap(other, mask) for mask in range(1, half)]
    return near + far


def joined(lse, axis):
    highest = jnp.max(lse, axis=axis, keepdims=True)
    return jnp.squeeze(highest, axis) + jnp.log(jnp.sum(jnp.exp(lse - highest), axis=axis))


def on_device(
    pictures,
    wordings,
    softness,
    queries,
    keys,
    values,
    img_owner,
    img_slot,
    txt_owner,
    txt_slot,
    img_cots,
    txt_cots,
):
    shape = jax.ShapeDtypeStruct
    n_txt = lax.axis_size("txt")
    place = jnp.stack([lax.axis_index("txt"), lax.axis_index("img")]).astype(jnp.int32)
    local, caption, width = queries.shape
    patches = keys.shape[1] - 1
    rows = (caption + 7) // 8 * 8
    everyone = n_txt * local
    slot_shape = (n_txt, local, caption, width)

    parts = gathered(queries, "txt")
    all_pictures = lax.all_gather(pictures, "txt", axis=0, tiled=True)
    sent = kernel_call(send_body, shape(slot_shape, BF16), 2, 1)(txt_owner, place, txt_cots)
    got_cots = lax.all_to_all(sent, "txt", 0, 0, tiled=True)

    pair_flops = 10 * caption * (patches + 1) * width
    sums = (
        shape((local, width, patches), F32),
        shape((local, width, patches), F32),
        shape((local, 1, width), F32),
        shape((local, 1, width), F32),
        shape((everyone, rows, width), F32),
    )
    img_pair_out, *partial = kernel_call(
        functools.partial(image_body, n_txt),
        (shape((local, NEGS, caption, width), BF16),) + sums,
        3,
        n_txt + 3,
        [pltpu.VMEM((everyone, rows, width), F32), pltpu.VMEM((local * NEGS, rows, width), F32)],
        flops=4 * local * NEGS * pair_flops,
        nbytes=10_000_000,
    )(img_owner, img_slot, place, *parts, img_cots, keys, values)

    row_stats, col_stats = kernel_call(
        contrast_body,
        (
            shape((all_pictures.shape[0] // LANES, 2, LANES), F32),
            shape((2, wordings.shape[0]), F32),
        ),
        2,
        2,
        [pltpu.VMEM(all_pictures.shape, BF16), pltpu.VMEM(wordings.shape, BF16)],
        flops=4 * all_pictures.shape[0] * wordings.shape[0] * 256,
        nbytes=1_000_000,
    )(place, softness, all_pictures, wordings)

    out, q_out, key_grad, value_grad = kernel_call(
        functools.partial(text_body, n_txt),
        (
            shape(slot_shape, BF16),
            shape(slot_shape, BF16),
            shape(keys.shape, BF16),
            shape(values.shape, BF16),
        ),
        3,
        n_txt + 8,
        [
            pltpu.VMEM((everyone + 1, rows, width), F32),
            pltpu.VMEM((everyone + 1, rows, width), F32),
            pltpu.VMEM((everyone + 1, rows, width), F32),
            *[pltpu.VMEM(s.shape, F32) for s in sums[:4]],
            pltpu.VMEM((everyone + 1, rows, width), F32),
            pltpu.SMEM((local, everyone + NEGS), jnp.int32),
            pltpu.SMEM((local,), jnp.int32),
        ],
        flops=4 * local * NEGS * pair_flops,
        nbytes=10_000_000,
    )(txt_owner, txt_slot, place, *parts, got_cots, keys, values, *partial)

    got_out = lax.all_to_all(out, "txt", 0, 0, tiled=True)
    got_q = lax.all_to_all(q_out, "txt", 0, 0, tiled=True)
    row_parts = row_stats.reshape(n_txt, -1, 2, LANES)
    got_rows = lax.all_to_all(row_parts, "txt", 0, 0, tiled=True)
    got_cols = lax.all_gather(col_stats, "img", axis=0)
    image_loss = (joined(got_rows[:, :, 0], 0) - jnp.sum(got_rows[:, :, 1], axis=0)).reshape(-1)
    text_loss = joined(got_cols[:, 0], 0) - jnp.sum(got_cols[:, 1], axis=0)
    txt_pair_out, query_grad = kernel_call(
        join_body, (shape(txt_cots.shape, BF16), shape(queries.shape, BF16)), 2, 2
    )(txt_owner, place, got_out, got_q)
    return (image_loss, text_loss, img_pair_out, txt_pair_out, query_grad, key_grad, value_grad)


def solution(mesh):
    every = ("img", "txt")
    three, four = P(every, None, None), P(every, None, None, None)
    table = P("img", None)
    return jax.shard_map(
        on_device,
        mesh=mesh,
        in_specs=(P(every, None), P("txt", None), P(), three, three, three)
        + (table, table, table, table, four, four),
        out_specs=(P(every), P("txt"), four, four, three, three, three),
        check_vma=False,
    )
```

```python
import functools

import jax
import jax.numpy as jnp
from jax import lax
from jax.experimental import pallas as pl
from jax.experimental.pallas import tpu as pltpu
from jax.sharding import PartitionSpec as P

NEGS = 4
EPSILON = 1e-06
LANES = 128
SMEM = pl.BlockSpec(memory_space=pltpu.SMEM)
ANY = pl.BlockSpec(memory_space=pl.ANY)
VMEM = pl.BlockSpec(memory_space=pltpu.VMEM)
F32 = jnp.float32
BF16 = jnp.bfloat16
NT = (((1,), (1,)), ((), ()))
TN = (((0,), (0,)), ((), ()))
NN = (((1,), (0,)), ((), ()))
CHUNK = 3


def kernel_call(body, out_shape, n_smem, n_any, scratch=(), flops=0, nbytes=0, space=ANY, mib=56, **more):
    return pl.pallas_call(
        body,
        out_shape=out_shape,
        in_specs=[SMEM] * n_smem + [space] * n_any,
        out_specs=jax.tree.map(lambda _: space, out_shape),
        scratch_shapes=list(scratch),
        compiler_params=pltpu.CompilerParams(vmem_limit_bytes=mib * 1024 * 1024),
        cost_estimate=pl.CostEstimate(flops=flops, bytes_accessed=nbytes, transcendentals=0),
        **more,
    )


def start_copies(pairs, sems, first=0):
    copies = [pltpu.make_async_copy(a, b, sems.at[first + n]) for n, (a, b) in enumerate(pairs)]
    for copy in copies:
        copy.start()
    return copies


def wait_copies(copies):
    for copy in copies:
        copy.wait()


def dot(a, b, dims):
    return lax.dot_general(a, b, dims, preferred_element_type=F32)


def padded(rows):
    return (rows + 7) // 8 * 8


def tie(value, *others):
    def body(*refs):
        del refs

    return kernel_call(
        body,
        jax.ShapeDtypeStruct(value.shape, value.dtype),
        0,
        1 + len(others),
        mib=1,
        input_output_aliases={0: 0},
    )(value, *others)


def pack_body(queries, pictures, packed):
    captions, caption = queries.shape[:2]
    first, emb = packed.shape[0] - fold_rows(pictures.shape, packed.shape[1]), pictures.shape[1]
    pieces = [queries[row].astype(F32) for row in range(captions)]
    pieces.append(jnp.zeros((first - captions * caption, packed.shape[1]), F32))
    packed[0:first, :] = jnp.concatenate(pieces, axis=0).astype(BF16)
    packed[first:, :] = jnp.zeros((packed.shape[0] - first, packed.shape[1]), BF16)
    for fold, (start, count) in enumerate(folds(pictures.shape, packed.shape[1])):
        packed[first : first + count, fold * emb : (fold + 1) * emb] = pictures[start : start + count]


def fold_rows(shape, width):
    return -(-shape[0] // (width // shape[1] * 16)) * 16


def folds(shape, width):
    step = fold_rows(shape, width)
    return [(start, min(step, shape[0] - start)) for start in range(0, shape[0], step)]


def named(tables, of_captions, row, entry):
    first = 2 * NEGS * of_captions
    return tables[first + entry, row], tables[first + NEGS + entry, row]


def send_body(tables, place, cots, sent):
    rows, caption = cots.shape[0], cots.shape[2]
    for part in range(sent.shape[0]):
        pieces = []
        for row in range(rows):
            at = jnp.int32(0)
            for entry in range(NEGS):
                owner, _ = named(tables, 1, place[0] * rows + row, entry)
                at = jnp.where(owner == part, entry, at)
            pieces.append(cots[row, at].astype(F32))
        pieces.append(jnp.zeros((sent.shape[1] - rows * caption, sent.shape[2]), F32))
        sent[part] = jnp.concatenate(pieces, axis=0).astype(BF16)


def contrast_body(n_parts, rows, place, softness, *refs):
    parts, refs = refs[:n_parts], refs[n_parts:]
    texts, row_out, col_out, held, texts_in, unit_images, unit_texts, row_stats, col_stats, sems = refs
    emb, step = texts_in.shape[1], held.shape[1]
    lines = pl.ds(parts[0].shape[0] - step, step)
    wait_copies(
        start_copies(
            [(texts, texts_in)] + [(parts[n].at[lines], held.at[n]) for n in range(n_parts)], sems
        )
    )

    def unit(source):
        wide = source.astype(F32)
        factor = lax.rsqrt(jnp.sum(wide * wide, axis=-1, keepdims=True) + EPSILON)
        return (wide * factor).astype(BF16)

    unit_texts[...] = unit(texts_in[...])
    for part in range(n_parts):
        first = jnp.bitwise_xor(part, place[0]) * rows
        for fold, (start, count) in enumerate(folds((rows, emb), held.shape[2])):
            at = pl.ds(pl.multiple_of(first + start, 16), count)
            unit_images[at, :] = unit(held[part, 0:count, fold * emb : (fold + 1) * emb])
    undo = 1.0 / softness[0]
    n_images, n_texts = n_parts * rows, texts_in.shape[0]
    first_image, first_text = place[1] * n_images, place[0] * n_texts

    def stats(long, long_first, short, short_first):
        logits = dot(long, short, NT) * undo
        highest = jnp.max(logits, axis=0, keepdims=True)
        total = jnp.sum(jnp.exp(logits - highest), axis=0, keepdims=True)
        on_diag = (lax.broadcasted_iota(jnp.int32, logits.shape, 0) + long_first) == (
            lax.broadcasted_iota(jnp.int32, logits.shape, 1) + short_first
        )
        diag = jnp.sum(jnp.where(on_diag, logits, 0.0), axis=0, keepdims=True)
        return highest + jnp.log(total), diag

    for block in range(n_parts):
        first = block * rows
        found = stats(
            unit_texts[...], first_text, unit_images[first : first + rows, :], first_image + first
        )
        at = 0
        for value in found:
            for _ in range(3):
                piece = value.astype(BF16).astype(F32)
                row_stats[block, :, at : at + rows] = piece
                value = value - piece
                at += rows
    for block in range(n_texts // LANES):
        first = block * LANES
        found = stats(
            unit_images[...], first_image, unit_texts[first : first + LANES, :], first_text + first
        )
        for n, value in enumerate(found):
            col_stats[n : n + 1, first : first + LANES] = value
    wait_copies(start_copies([(row_stats, row_out), (col_stats, col_out)], sems))


def attend(chunks, queries, cots, keys, values, sums):
    half = LANES // 2
    tiles = [slice(n * LANES, (n + 1) * LANES) for n in range(keys.shape[2] // LANES)]
    work = [(chunk, lanes) for chunk in chunks for lanes in tiles]

    def stacked(ref, at, lanes):
        pieces = [ref[n, :, lanes] for n in at]
        pieces.append(jnp.zeros((LANES - len(at) * ref.shape[1], LANES), F32))
        tile = jnp.concatenate(pieces, axis=0)
        low = lax.broadcasted_iota(jnp.int32, tile.shape, 1) < half
        pair = jnp.concatenate([jnp.where(low, tile, 0.0), jnp.where(low, 0.0, tile)], axis=0)
        return pair.astype(BF16)

    def folded(pair):
        return jnp.transpose(jnp.concatenate([pair[:half, :LANES], pair[half:, LANES:]], axis=0))

    q = [stacked(queries, chunk[1], lanes) for chunk, lanes in work]
    logits = [dot(keys[chunk[0], :, lanes], q[n], NT) for n, (chunk, lanes) in enumerate(work)]
    if cots is not None:
        g = [stacked(cots, chunk[2], lanes) for chunk, lanes in work]
        terms = [dot(values[chunk[0], :, lanes], g[n], NT) for n, (chunk, lanes) in enumerate(work)]
    weights = []
    for logit in logits:
        shifted = jnp.exp(logit - jnp.max(logit, axis=0, keepdims=True))
        weights.append(shifted * (1.0 / jnp.sum(shifted, axis=0, keepdims=True)))
    rounded = [weight.astype(BF16) for weight in weights]
    outputs = [
        dot(values[chunk[0], :, lanes], rounded[n], TN) if chunk[3] is not None else None
        for n, (chunk, lanes) in enumerate(work)
    ]
    if cots is not None:
        key_sum, value_sum = sums
        value_terms = [dot(rounded[n], g[n], NN) for n in range(len(work))]
        logit_terms = []
        for weight, term in zip(weights, terms):
            inner = jnp.sum(weight * term, axis=0, keepdims=True)
            logit_terms.append((weight * (term - inner)).astype(BF16))
        q_terms = [dot(keys[chunk[0], :, lanes], logit_terms[n], TN) for n, (chunk, lanes) in enumerate(work)]
        key_terms = [dot(logit_terms[n], q[n], NN) for n in range(len(work))]
        for n, (chunk, lanes) in enumerate(work):
            key_sum[chunk[0], :, lanes] += key_terms[n]
            value_sum[chunk[0], :, lanes] += value_terms[n]
    for n, (chunk, lanes) in enumerate(work):
        if chunk[3] is not None:
            chunk[3](lanes, folded(outputs[n]))
        if chunk[4] is not None:
            chunk[4](lanes, folded(q_terms[n]) * 0.125)


def widen(source, wide, at, scale=1.0):
    caption = source.shape[0]
    wide[at, caption:, :] = jnp.zeros((wide.shape[1] - caption, wide.shape[2]), F32)
    wide[at, 0:caption, :] = source.astype(F32) * scale


def query_copies(parts, held):
    lines = pl.ds(0, held.shape[1])
    return [(part.at[lines], held.at[n]) for n, part in enumerate(parts)]


def widen_block(block, wide, first, captions, caption):
    for row in range(captions):
        wide[first + row, caption:, :] = jnp.zeros((wide.shape[1] - caption, wide.shape[2]), F32)
        wide[first + row, 0:caption, :] = block[row * caption : (row + 1) * caption]


def widen_queries(held, queries, captions, caption):
    n_parts = held.shape[0]
    for part in range(n_parts):
        widen_block(held[part].astype(F32) * 0.125, queries, part * captions, captions, caption)
    if queries.shape[0] > n_parts * captions:
        queries[n_parts * captions] = jnp.zeros(queries.shape[1:], F32)


def find_listed(tables, place, lists, counts, everyone):
    for image in range(counts.shape[0]):
        counts[image] = 0

        def clear(i, _, image=image):
            lists[image, i] = everyone
            return 0

        lax.fori_loop(0, lists.shape[1], clear, 0)

    def find(j, _):
        for entry in range(NEGS):
            owner, image = named(tables, 1, j, entry)

            @pl.when(owner == place[0])
            def _():
                lists[image, counts[image]] = j
                counts[image] = counts[image] + 1

        return 0

    lax.fori_loop(0, everyone, find, 0)


def each_pair_of_chunks(lists, counts, place, captions, everyone, work):
    images = counts.shape[0]
    needed = [(counts[image] + CHUNK - 1) // CHUNK for image in range(images)]

    def pair_step(pair, _):
        chunks = []
        for n in range(2):
            chunk = 2 * pair + n
            image, first, past = jnp.int32(0), jnp.int32(0), jnp.int32(0)
            for later in range(1, images):
                past = past + needed[later - 1]
                image = jnp.where(chunk >= past, later, image)
                first = jnp.where(chunk >= past, past, first)
            j = [lists[image, (chunk - first) * CHUNK + e] for e in range(CHUNK)]
            q_at = [
                jnp.where(
                    n < everyone,
                    jnp.bitwise_xor(n // captions, place[0]) * captions + n % captions,
                    everyone,
                )
                for n in j
            ]
            chunks.append((image, j, q_at))
        work(chunks)
        return 0

    lax.fori_loop(0, (sum(needed) + 1) // 2, pair_step, 0)


def image_body(n_parts, tables, place, *refs):
    parts, refs = refs[:n_parts], refs[n_parts:]
    (cots_in, keys_in, values_in, image_out, image_terms, key_out, value_out, text_out,
     held, queries, cots_held, cots, keys, values, image_outs, terms, sums, outs, blocks,
     lists, counts, sems) = refs
    images = captions = keys.shape[0]
    caption = cots_held.shape[2]
    rows = queries.shape[1]
    everyone = n_parts * captions
    copies = start_copies(
        query_copies(parts, held) + [(cots_in, cots_held), (keys_in, keys), (values_in, values)], sems
    )
    find_listed(tables, place, lists, counts, everyone)
    for total in (*sums, outs):
        total[...] = jnp.zeros_like(total)
    wait_copies(copies)
    widen_queries(held, queries, captions, caption)
    for image in range(images):
        for entry in range(NEGS):
            widen(cots_held[image, entry], cots, image * NEGS + entry)
    for first in range(0, NEGS, CHUNK):
        entries = range(first, min(first + CHUNK, NEGS))
        chunks = []
        for image in range(images):
            at = []
            for entry in entries:
                owner, slot = named(tables, 0, place[0] * images + image, entry)
                at.append(jnp.bitwise_xor(owner, place[0]) * captions + slot)

            def emit(ref, lanes, value, image=image, entries=entries):
                for n, e in enumerate(entries):
                    ref[image, e, :, lanes] = value[n * rows : n * rows + caption].astype(BF16)

            chunks.append(
                (
                    image, at, [image * NEGS + e for e in entries],
                    functools.partial(emit, image_outs), functools.partial(emit, terms),
                )
            )
        attend(chunks, queries, cots, keys, values, sums)
    copies = start_copies(
        [(image_outs, image_out), (terms, image_terms), *zip(sums, (key_out, value_out))], sems
    )

    def work(chunks):
        def emit_out(j, lanes, output):
            for e in range(CHUNK):
                outs[j[e], :, lanes] = output[e * rows : (e + 1) * rows]

        attend(
            [
                (image, q_at, None, functools.partial(emit_out, j), None)
                for image, j, q_at in chunks
            ],
            queries, None, keys, values, None,
        )

    each_pair_of_chunks(lists, counts, place, captions, everyone, work)
    for part in range(n_parts):
        pieces = [outs[part * captions + row, 0:caption, :] for row in range(captions)]
        pieces.append(jnp.zeros((blocks.shape[1] - captions * caption, blocks.shape[2]), F32))
        blocks[part] = jnp.concatenate(pieces, axis=0).astype(BF16)
        copies += start_copies([(blocks.at[part], text_out.at[part])], sems, 4 + part)
    wait_copies(copies)


def text_body(n_parts, tables, place, *refs):
    parts, refs = refs[:n_parts], refs[n_parts:]
    (cots_in, keys_in, values_in, stats_in, terms_in, key_in, value_in, q_out, key_grad, value_grad,
     held, queries, cots_held, cots, keys, values, stats, terms, q_sum, firsts, sums, grads,
     lists, counts, sems) = refs
    images = captions = keys.shape[0]
    caption = terms.shape[2]
    rows = queries.shape[1]
    everyone = n_parts * captions
    copies = start_copies(
        query_copies(parts, held) + [(cots_in, cots_held), (keys_in, keys), (values_in, values)], sems
    )
    later = start_copies(
        [(stats_in, stats), (terms_in, terms), *zip((key_in, value_in), firsts)], sems, len(copies)
    )
    find_listed(tables, place, lists, counts, everyone)
    for total in (*sums, q_sum):
        total[...] = jnp.zeros_like(total)
    wait_copies(copies)
    widen_queries(held, queries, captions, caption)
    for part in range(n_parts):
        widen_block(cots_held[part].astype(F32), cots, part * captions, captions, caption)
    cots[everyone] = jnp.zeros(cots.shape[1:], F32)

    def work(chunks):
        def emit_q(q_at, lanes, term):
            for e in range(CHUNK):
                q_sum[q_at[e], :, lanes] += term[e * rows : (e + 1) * rows].astype(BF16).astype(F32)

        attend(
            [(image, q_at, j, None, functools.partial(emit_q, q_at)) for image, j, q_at in chunks],
            queries, cots, keys, values, sums,
        )

    each_pair_of_chunks(lists, counts, place, captions, everyone, work)
    wait_copies(later)
    for image in range(images):
        for entry in range(NEGS):
            owner, slot = named(tables, 0, place[0] * images + image, entry)
            at = jnp.bitwise_xor(owner, place[0]) * captions + slot
            q_sum[at, 0:caption, :] += terms[image, entry].astype(F32)
    out = []
    for part in range(n_parts):
        first = jnp.bitwise_xor(part, place[0]) * captions
        pieces = [q_sum[first + row, 0:caption, :] for row in range(captions)]
        pieces.append(stats[part])
        pieces.append(jnp.zeros((cots_held.shape[1] - captions * caption - 1, stats.shape[2]), F32))
        cots_held[part] = jnp.concatenate(pieces, axis=0).astype(BF16)
        out += start_copies([(cots_held.at[part], q_out.at[part])], sems, part)
    for n, grad in enumerate((key_grad, value_grad)):
        for image in range(images):
            grads[n][image] = (sums[n][image] + firsts[n][image]).astype(BF16)
        out += start_copies([(grads[n], grad)], sems, n_parts + n)
    wait_copies(out)


def join_body(tables, place, got_out, got_q, cols, pair_out, q_grad, image_loss, text_loss):
    rows, caption = pair_out.shape[0], pair_out.shape[2]
    n_parts = got_q.shape[0]
    for row in range(rows):
        lines = slice(row * caption, (row + 1) * caption)
        for entry in range(NEGS):
            owner, _ = named(tables, 1, place[0] * rows + row, entry)
            block = got_out[owner].astype(F32)
            pair_out[row, entry] = block[lines].astype(BF16)
    total = got_q[0].astype(F32)
    for source in range(1, n_parts):
        total = total + got_q[source].astype(F32)
    for row in range(rows):
        q_grad[row] = total[row * caption : (row + 1) * caption].astype(BF16)

    def joined(parts):
        highest = functools.reduce(jnp.maximum, parts)
        return highest + jnp.log(sum(jnp.exp(part - highest) for part in parts))

    width = image_loss.shape[1]
    line = rows * caption
    lse, diag = [], jnp.zeros(image_loss.shape, F32)
    for source in range(n_parts):
        stats = got_q[source].astype(F32)[line : line + 1]
        pieces = [stats[:, n * width : (n + 1) * width] for n in range(6)]
        lse.append(pieces[0] + pieces[1] + pieces[2])
        diag = diag + (pieces[3] + pieces[4] + pieces[5])
    image_loss[...] = joined(lse) - diag
    n_cols = cols.shape[0]
    text_loss[...] = joined([cols[n, 0:1, :] for n in range(n_cols)]) - sum(
        cols[n, 1:2, :] for n in range(n_cols)
    )


def swap(part, axis, mask):
    return lax.ppermute(part, axis, [(s, s ^ mask) for s in range(lax.axis_size(axis))])


def gathered(block, axis):
    half = lax.axis_size(axis) // 2
    other = swap(block, axis, half)
    near = [block] + [swap(block, axis, mask) for mask in range(1, half)]
    far = [other] + [swap(other, axis, mask) for mask in range(1, half)]
    return near + far


def on_device(
    pictures,
    wordings,
    softness,
    queries,
    keys,
    values,
    img_owner,
    img_slot,
    txt_owner,
    txt_slot,
    img_cots,
    txt_cots,
):
    shape = jax.ShapeDtypeStruct
    vmem = pltpu.VMEM
    dma = lambda n: pltpu.SemaphoreType.DMA((n,))
    n_txt = lax.axis_size("txt")
    place = jnp.stack([lax.axis_index("txt"), lax.axis_index("img")]).astype(jnp.int32)
    local, caption, width = queries.shape
    patches = keys.shape[1]
    rows = padded(caption)
    everyone = n_txt * local
    block_shape = (n_txt, padded(local * caption + 1), width)
    wide_shape = (everyone + 1, rows, width)
    query_rows = -(-local * caption // 16) * 16
    held_shape = (n_txt, query_rows, width)
    pair_flops = 10 * caption * patches * width
    tables = jnp.concatenate([table.T for table in (img_owner, img_slot, txt_owner, txt_slot)], axis=0)
    sums = [vmem(keys.shape, F32), vmem(values.shape, F32)]
    lists = [pltpu.SMEM((local, everyone + 2 * CHUNK), jnp.int32), pltpu.SMEM((local,), jnp.int32)]

    step = fold_rows(pictures.shape, width)
    packed = kernel_call(pack_body, shape((query_rows + step, width), BF16), 0, 2, space=VMEM, mib=8)(
        queries, pictures
    )
    parts = gathered(packed, "txt")
    sent = kernel_call(send_body, shape(block_shape, BF16), 2, 1, space=VMEM, mib=12)(
        tables, place, txt_cots
    )
    ready = parts[1 : n_txt // 2] + parts[n_txt // 2 + 1 :]
    got_cots = lax.all_to_all(tie(sent, *ready, keys, values, img_cots), "txt", 0, 0, tiled=True)

    img_pair_out, image_terms, key_part, value_part, out = kernel_call(
        functools.partial(image_body, n_txt),
        (
            shape(img_cots.shape, BF16),
            shape(img_cots.shape, BF16),
            shape(keys.shape, F32),
            shape(values.shape, F32),
            shape(block_shape, BF16),
        ),
        2,
        n_txt + 3,
        [
            vmem(held_shape, BF16),
            vmem(wide_shape, F32),
            vmem(img_cots.shape, BF16),
            vmem((local * NEGS, rows, width), F32),
            vmem(keys.shape, BF16),
            vmem(values.shape, BF16),
            vmem(img_cots.shape, BF16),
            vmem(img_cots.shape, BF16),
            sums,
            vmem(wide_shape, F32),
            vmem(block_shape, BF16),
            *lists,
            dma(n_txt + 4),
        ],
        flops=6 * local * NEGS * pair_flops,
        nbytes=12_000_000,
    )(tables, place, *parts, img_cots, keys, values)
    got_out = lax.all_to_all(out, "txt", 0, 0, tiled=True)

    image_rows, n_texts, emb = pictures.shape[0], wordings.shape[0], wordings.shape[1]
    stats_shape = (n_txt, 1, 6 * image_rows)
    row_stats, col_stats = kernel_call(
        functools.partial(contrast_body, n_txt, image_rows),
        (shape(stats_shape, F32), shape((2, n_texts), F32)),
        2,
        n_txt + 1,
        [
            vmem((n_txt, step, width), BF16),
            vmem(wordings.shape, BF16),
            vmem((n_txt * image_rows, emb), BF16),
            vmem(wordings.shape, BF16),
            vmem(stats_shape, F32),
            vmem((2, n_texts), F32),
            dma(n_txt + 1),
        ],
        flops=4 * n_txt * image_rows * n_texts * emb,
        nbytes=1_000_000,
    )(place, softness, *parts, wordings)
    got_cols = lax.all_gather(col_stats, "img", axis=0)

    q_out, key_grad, value_grad = kernel_call(
        functools.partial(text_body, n_txt),
        (shape(block_shape, BF16), shape(keys.shape, BF16), shape(values.shape, BF16)),
        2,
        n_txt + 7,
        [
            vmem(held_shape, BF16),
            vmem(wide_shape, F32),
            vmem(block_shape, BF16),
            vmem(wide_shape, F32),
            vmem(keys.shape, BF16),
            vmem(values.shape, BF16),
            vmem(stats_shape, F32),
            vmem(img_cots.shape, BF16),
            vmem(wide_shape, F32),
            sums,
            sums,
            [vmem(keys.shape, BF16), vmem(values.shape, BF16)],
            *lists,
            dma(n_txt + 7),
        ],
        flops=4 * local * NEGS * pair_flops,
        nbytes=10_000_000,
    )(tables, place, *parts, got_cots, keys, values, row_stats, image_terms, key_part, value_part)
    got_q = lax.all_to_all(q_out, "txt", 0, 0, tiled=True)

    txt_pair_out, query_grad, image_loss, text_loss = kernel_call(
        join_body,
        (
            shape(txt_cots.shape, BF16),
            shape(queries.shape, BF16),
            shape((1, image_rows), F32),
            shape((1, n_texts), F32),
        ),
        2,
        3,
        space=VMEM,
        mib=16,
    )(tables, place, got_out, got_q, got_cols)
    return (
        image_loss.reshape(-1),
        text_loss.reshape(-1),
        img_pair_out,
        txt_pair_out,
        query_grad,
        key_grad,
        value_grad,
    )


def solution(mesh):
    every = ("img", "txt")
    three, four = P(every, None, None), P(every, None, None, None)
    table = P("img", None)
    return jax.shard_map(
        on_device,
        mesh=mesh,
        in_specs=(P(every, None), P("txt", None), P(), three, three, three)
        + (table, table, table, table, four, four),
        out_specs=(P(every), P("txt"), four, four, three, three, three),
        check_vma=False,
    )
```

```python
import functools

import jax
import jax.numpy as jnp
from jax import lax
from jax.experimental import pallas as pl
from jax.experimental.pallas import tpu as pltpu
from jax.sharding import PartitionSpec as P

NEGS = 4
EPSILON = 1e-06
LANES = 128
SMEM = pl.BlockSpec(memory_space=pltpu.SMEM)
ANY = pl.BlockSpec(memory_space=pl.ANY)
VMEM = pl.BlockSpec(memory_space=pltpu.VMEM)
F32 = jnp.float32
BF16 = jnp.bfloat16
NT = (((1,), (1,)), ((), ()))
TN = (((0,), (0,)), ((), ()))
NN = (((1,), (0,)), ((), ()))
CHUNK = 3


def kernel_call(body, out_shape, n_smem, n_any, scratch=(), flops=0, nbytes=0, space=ANY, mib=60, n_after=0, **more):
    return pl.pallas_call(
        body,
        out_shape=out_shape,
        in_specs=[SMEM] * n_smem + [space] * n_any + [ANY] * n_after,
        out_specs=jax.tree.map(lambda _: space, out_shape),
        scratch_shapes=list(scratch),
        compiler_params=pltpu.CompilerParams(vmem_limit_bytes=mib * 1024 * 1024),
        cost_estimate=pl.CostEstimate(flops=flops, bytes_accessed=nbytes, transcendentals=0),
        **more,
    )


def start_copies(pairs, sems, first=0):
    copies = [pltpu.make_async_copy(a, b, sems.at[first + n]) for n, (a, b) in enumerate(pairs)]
    for copy in copies:
        copy.start()
    return copies


def wait_copies(copies):
    for copy in copies:
        copy.wait()


def dot(a, b, dims):
    return lax.dot_general(a, b, dims, preferred_element_type=F32)


def padded(rows):
    return (rows + 7) // 8 * 8


def tie(value, *others):
    def body(*refs):
        del refs

    return kernel_call(
        body,
        jax.ShapeDtypeStruct(value.shape, value.dtype),
        0,
        1 + len(others),
        input_output_aliases={0: 0},
    )(value, *others)


def pack_body(queries, pictures, packed, both):
    captions, caption = queries.shape[:2]
    first, emb = packed.shape[0], pictures.shape[1]
    pieces = [queries[row].astype(F32) for row in range(captions)]
    pieces.append(jnp.zeros((first - captions * caption, packed.shape[1]), F32))
    packed[...] = jnp.concatenate(pieces, axis=0).astype(BF16)
    both[0:first, :] = packed[...]
    both[first:, :] = jnp.zeros((both.shape[0] - first, packed.shape[1]), BF16)
    for fold, (start, count) in enumerate(folds(pictures.shape, packed.shape[1])):
        both[first : first + count, fold * emb : (fold + 1) * emb] = pictures[start : start + count]


def fold_rows(shape, width):
    return -(-shape[0] // (width // shape[1] * 16)) * 16


def folds(shape, width):
    step = fold_rows(shape, width)
    return [(start, min(step, shape[0] - start)) for start in range(0, shape[0], step)]


def named(tables, of_captions, row, entry):
    first = 2 * NEGS * of_captions
    return tables[first + entry, row], tables[first + NEGS + entry, row]


def send_body(tables, place, cots, *refs):
    sent = refs[-1]
    rows, caption = cots.shape[0], cots.shape[2]
    for part in range(sent.shape[0]):
        pieces = []
        for row in range(rows):
            at = jnp.int32(0)
            for entry in range(NEGS):
                owner, _ = named(tables, 1, place[0] * rows + row, entry)
                at = jnp.where(owner == part, entry, at)
            pieces.append(cots[row, at].astype(F32))
        pieces.append(jnp.zeros((sent.shape[1] - rows * caption, sent.shape[2]), F32))
        sent[part] = jnp.concatenate(pieces, axis=0).astype(BF16)


def in_pieces(values):
    pieces = []
    for value in values:
        for _ in range(3):
            pieces.append(value.astype(BF16).astype(F32))
            value = value - pieces[-1]
    return jnp.concatenate(pieces, axis=1)


def from_pieces(line):
    width = line.shape[1] // 6
    pieces = [line[:, n * width : (n + 1) * width] for n in range(6)]
    return pieces[0] + pieces[1] + pieces[2], pieces[3] + pieces[4] + pieces[5]


def joined(parts):
    highest = functools.reduce(jnp.maximum, parts)
    return highest + jnp.log(sum(jnp.exp(part - highest) for part in parts))


def contrast(n_parts, place, softness, near_in, images_in, texts_in, unit_images, unit_texts, row_stats, col_stats):
    rows, emb = images_in.shape[1:]

    def unit(source):
        wide = source.astype(F32)
        factor = lax.rsqrt(jnp.sum(wide * wide, axis=-1, keepdims=True) + EPSILON)
        return (wide * factor).astype(BF16)

    unit_texts[...] = unit(texts_in[...])
    for part in range(n_parts // 2):
        for fold, (start, count) in enumerate(folds((rows, emb), near_in.shape[2])):
            images_in[part, start : start + count, :] = near_in[part, 0:count, fold * emb : (fold + 1) * emb]
    for part in range(n_parts):
        first = jnp.bitwise_xor(part, place[0]) * rows
        unit_images[pl.ds(pl.multiple_of(first, 16), rows), :] = unit(images_in[part])
    undo = 1.0 / softness[0]
    n_images, n_texts = n_parts * rows, texts_in.shape[0]
    first_image, first_text = place[1] * n_images, place[0] * n_texts

    def stats(long, long_first, short, short_first, count):
        blocks = range(0, short.shape[0], count)
        logits = [dot(long[...], short[at : at + count, :], NT) * undo for at in blocks]
        highest = [jnp.max(block, axis=0, keepdims=True) for block in logits]
        total = [
            jnp.sum(jnp.exp(block - top), axis=0, keepdims=True) for block, top in zip(logits, highest)
        ]
        for at, block, top, whole in zip(blocks, logits, highest, total):
            on_diag = (lax.broadcasted_iota(jnp.int32, block.shape, 0) + long_first) == (
                lax.broadcasted_iota(jnp.int32, block.shape, 1) + (short_first + at)
            )
            diag = jnp.sum(jnp.where(on_diag, block, 0.0), axis=0, keepdims=True)
            yield at, (top + jnp.log(whole), diag)

    for at, found in stats(unit_texts, first_text, unit_images, first_image, rows):
        row_stats[at // rows] = in_pieces(found)
    for at, found in stats(unit_images, first_image, unit_texts, first_text, LANES):
        for n, value in enumerate(found):
            col_stats[n : n + 1, at : at + LANES] = value


def attend(chunks, queries, cots, keys, values, sums):
    half = LANES // 2
    tiles = [slice(n * LANES, (n + 1) * LANES) for n in range(keys.shape[2] // LANES)]
    work = [(chunk, lanes) for chunk in chunks for lanes in tiles]

    def stacked(ref, at, lanes):
        pieces = [ref[n, :, lanes] for n in at]
        pieces.append(jnp.zeros((LANES - len(at) * ref.shape[1], LANES), F32))
        tile = jnp.concatenate(pieces, axis=0)
        low = lax.broadcasted_iota(jnp.int32, tile.shape, 1) < half
        pair = jnp.concatenate([jnp.where(low, tile, 0.0), jnp.where(low, 0.0, tile)], axis=0)
        return pair.astype(BF16)

    def folded(pair):
        return jnp.transpose(jnp.concatenate([pair[:half, :LANES], pair[half:, LANES:]], axis=0))

    q = [stacked(queries, chunk[1], lanes) for chunk, lanes in work]
    logits = [dot(keys[chunk[0], :, lanes], q[n], NT) for n, (chunk, lanes) in enumerate(work)]
    if cots is not None:
        g = [stacked(cots, chunk[2], lanes) for chunk, lanes in work]
        terms = [dot(values[chunk[0], :, lanes], g[n], NT) for n, (chunk, lanes) in enumerate(work)]
    weights = []
    for logit in logits:
        shifted = jnp.exp(logit - jnp.max(logit, axis=0, keepdims=True))
        weights.append(shifted * (1.0 / jnp.sum(shifted, axis=0, keepdims=True)))
    rounded = [weight.astype(BF16) for weight in weights]
    outputs = [
        dot(values[chunk[0], :, lanes], rounded[n], TN) if chunk[3] is not None else None
        for n, (chunk, lanes) in enumerate(work)
    ]
    if cots is not None:
        key_sum, value_sum = sums
        value_terms = [dot(rounded[n], g[n], NN) for n in range(len(work))]
        logit_terms = []
        for weight, term in zip(weights, terms):
            inner = jnp.sum(weight * term, axis=0, keepdims=True)
            logit_terms.append((weight * (term - inner)).astype(BF16))
        q_terms = [dot(keys[chunk[0], :, lanes], logit_terms[n], TN) for n, (chunk, lanes) in enumerate(work)]
        key_terms = [dot(logit_terms[n], q[n], NN) for n in range(len(work))]
        for n, (chunk, lanes) in enumerate(work):
            key_sum[chunk[0], :, lanes] += key_terms[n]
            value_sum[chunk[0], :, lanes] += value_terms[n]
    for n, (chunk, lanes) in enumerate(work):
        if chunk[3] is not None:
            chunk[3](lanes, folded(outputs[n]))
        if chunk[4] is not None:
            chunk[4](lanes, folded(q_terms[n]) * 0.125)


def widen(source, wide, at, scale=1.0):
    caption = source.shape[0]
    wide[at, caption:, :] = jnp.zeros((wide.shape[1] - caption, wide.shape[2]), F32)
    wide[at, 0:caption, :] = source.astype(F32) * scale


def query_copies(parts, held):
    lines = pl.ds(0, held.shape[1])
    return [(part.at[lines], held.at[n]) for n, part in enumerate(parts)]


def widen_block(block, wide, first, captions, caption):
    for row in range(captions):
        wide[first + row, caption:, :] = jnp.zeros((wide.shape[1] - caption, wide.shape[2]), F32)
        wide[first + row, 0:caption, :] = block[row * caption : (row + 1) * caption]


def widen_queries(held, queries, captions, caption):
    n_parts = held.shape[0]
    for part in range(n_parts):
        widen_block(held[part].astype(F32) * 0.125, queries, part * captions, captions, caption)
    if queries.shape[0] > n_parts * captions:
        queries[n_parts * captions] = jnp.zeros(queries.shape[1:], F32)


def find_listed(tables, place, lists, counts, everyone):
    for image in range(counts.shape[0]):
        counts[image] = 0

        def clear(i, _, image=image):
            lists[image, i] = everyone
            return 0

        lax.fori_loop(0, lists.shape[1], clear, 0)

    def find(j, _):
        for entry in range(NEGS):
            owner, image = named(tables, 1, j, entry)

            @pl.when(owner == place[0])
            def _():
                lists[image, counts[image]] = j
                counts[image] = counts[image] + 1

        return 0

    lax.fori_loop(0, everyone, find, 0)


def each_pair_of_chunks(lists, counts, place, captions, everyone, work):
    images = counts.shape[0]
    needed = [(counts[image] + CHUNK - 1) // CHUNK for image in range(images)]

    def pair_step(pair, _):
        chunks = []
        for n in range(2):
            chunk = 2 * pair + n
            image, first, past = jnp.int32(0), jnp.int32(0), jnp.int32(0)
            for later in range(1, images):
                past = past + needed[later - 1]
                image = jnp.where(chunk >= past, later, image)
                first = jnp.where(chunk >= past, past, first)
            j = [lists[image, (chunk - first) * CHUNK + e] for e in range(CHUNK)]
            q_at = [
                jnp.where(
                    n < everyone,
                    jnp.bitwise_xor(n // captions, place[0]) * captions + n % captions,
                    everyone,
                )
                for n in j
            ]
            chunks.append((image, j, q_at))
        work(chunks)
        return 0

    lax.fori_loop(0, (sum(needed) + 1) // 2, pair_step, 0)


def image_body(n_parts, tables, place, *refs):
    parts, refs = refs[:n_parts], refs[n_parts:]
    (cots_in, keys_in, values_in, image_out, image_terms, key_out, value_out, text_out,
     held, queries, cots_held, cots, keys, values, image_outs, terms, sums, outs, blocks,
     lists, counts, sems) = refs
    images = captions = keys.shape[0]
    caption = cots_held.shape[2]
    rows = queries.shape[1]
    everyone = n_parts * captions
    copies = start_copies(
        query_copies(parts, held) + [(cots_in, cots_held), (keys_in, keys), (values_in, values)], sems
    )
    find_listed(tables, place, lists, counts, everyone)
    for total in (*sums, outs):
        total[...] = jnp.zeros_like(total)
    wait_copies(copies)
    widen_queries(held, queries, captions, caption)
    for image in range(images):
        for entry in range(NEGS):
            widen(cots_held[image, entry], cots, image * NEGS + entry)
    for first in range(0, NEGS, CHUNK):
        entries = range(first, min(first + CHUNK, NEGS))
        chunks = []
        for image in range(images):
            at = []
            for entry in entries:
                owner, slot = named(tables, 0, place[0] * images + image, entry)
                at.append(jnp.bitwise_xor(owner, place[0]) * captions + slot)

            def emit(ref, lanes, value, image=image, entries=entries):
                for n, e in enumerate(entries):
                    ref[image, e, :, lanes] = value[n * rows : n * rows + caption].astype(BF16)

            chunks.append(
                (
                    image, at, [image * NEGS + e for e in entries],
                    functools.partial(emit, image_outs), functools.partial(emit, terms),
                )
            )
        attend(chunks, queries, cots, keys, values, sums)
    copies = start_copies(
        [(image_outs, image_out), (terms, image_terms), *zip(sums, (key_out, value_out))], sems
    )

    def work(chunks):
        def emit_out(j, lanes, output):
            for e in range(CHUNK):
                outs[j[e], :, lanes] = output[e * rows : (e + 1) * rows]

        attend(
            [
                (image, q_at, None, functools.partial(emit_out, j), None)
                for image, j, q_at in chunks
            ],
            queries, None, keys, values, None,
        )

    each_pair_of_chunks(lists, counts, place, captions, everyone, work)
    for part in range(n_parts):
        pieces = [outs[part * captions + row, 0:caption, :] for row in range(captions)]
        pieces.append(jnp.zeros((blocks.shape[1] - captions * caption, blocks.shape[2]), F32))
        blocks[part] = jnp.concatenate(pieces, axis=0).astype(BF16)
        copies += start_copies([(blocks.at[part], text_out.at[part])], sems, 4 + part)
    wait_copies(copies)


def text_body(n_parts, tables, place, softness, *refs):
    half = n_parts // 2
    parts, pictures, refs = refs[:n_parts], refs[n_parts : n_parts + half], refs[n_parts + half :]
    (texts, cots_in, keys_in, values_in, terms_in, key_in, value_in), refs = refs[:7], refs[7:]
    q_out, refs = refs[:half], refs[half:]
    (key_grad, value_grad, col_out,
     held, queries, cots_held, cots, keys, values, terms, q_sum, firsts, sums, grads,
     near_in, images_in, texts_in, unit_images, unit_texts, row_stats, col_stats, lists, counts, sems) = refs
    images = captions = keys.shape[0]
    caption = terms.shape[2]
    rows = queries.shape[1]
    everyone = n_parts * captions
    soon = start_copies(
        [(texts, texts_in)]
        + [(part.at[pl.ds(held.shape[1], near_in.shape[1])], near_in.at[n]) for n, part in enumerate(parts[:half])]
        + [(picture, images_in.at[half + n]) for n, picture in enumerate(pictures)],
        sems,
    )
    copies = start_copies(
        query_copies(parts, held) + [(cots_in, cots_held), (keys_in, keys), (values_in, values)],
        sems,
        len(soon),
    )
    find_listed(tables, place, lists, counts, everyone)
    for total in (*sums, q_sum):
        total[...] = jnp.zeros_like(total)
    wait_copies(soon)
    contrast(
        n_parts, place, softness, near_in, images_in, texts_in, unit_images, unit_texts, row_stats, col_stats
    )
    wait_copies(copies)
    later = start_copies([(terms_in, terms), *zip((key_in, value_in), firsts)], sems)
    out = start_copies([(col_stats, col_out)], sems, len(soon))
    widen_queries(held, queries, captions, caption)
    for part in range(n_parts):
        widen_block(cots_held[part].astype(F32), cots, part * captions, captions, caption)
    cots[everyone] = jnp.zeros(cots.shape[1:], F32)

    def work(chunks):
        def emit_q(q_at, lanes, term):
            for e in range(CHUNK):
                q_sum[q_at[e], :, lanes] += term[e * rows : (e + 1) * rows].astype(BF16).astype(F32)

        attend(
            [(image, q_at, j, None, functools.partial(emit_q, q_at)) for image, j, q_at in chunks],
            queries, cots, keys, values, sums,
        )

    each_pair_of_chunks(lists, counts, place, captions, everyone, work)
    wait_copies(later)
    for image in range(images):
        for entry in range(NEGS):
            owner, slot = named(tables, 0, place[0] * images + image, entry)
            at = jnp.bitwise_xor(owner, place[0]) * captions + slot
            q_sum[at, 0:caption, :] += terms[image, entry].astype(F32)
    block_rows = cots_held.shape[1]
    for part in range(n_parts):
        target = jnp.bitwise_xor(part, place[0])
        pieces = [q_sum[part * captions + row, 0:caption, :] for row in range(captions)]
        pieces.append(row_stats[target])
        pieces.append(jnp.zeros((block_rows - captions * caption - 1, cots_held.shape[2]), F32))
        cots_held[part] = jnp.concatenate(pieces, axis=0).astype(BF16)
        out += start_copies([(cots_held.at[part], q_out[part % half].at[part // half])], sems, part)
    for n, grad in enumerate((key_grad, value_grad)):
        for image in range(images):
            grads[n][image] = (sums[n][image] + firsts[n][image]).astype(BF16)
        out += start_copies([(grads[n], grad)], sems, n_parts + n)
    wait_copies(out)


def add_lines(blocks, lines):
    total = blocks[0].astype(F32)
    for block in blocks[1:]:
        total = total + block.astype(F32)
    found = [from_pieces(block[lines : lines + 1].astype(F32)) for block in blocks]
    return total[0:lines], joined([lse for lse, _ in found]), sum(diag for _, diag in found)


def half_body(lines, after, *refs):
    del after
    blocks, kept, sent = refs[:-2], refs[-2], refs[-1]
    for side, out in enumerate((kept, sent)):
        total, lse, diag = add_lines([block[side] for block in blocks], lines)
        rest = jnp.zeros((out.shape[0] - lines - 1, out.shape[1]), F32)
        out[...] = jnp.concatenate([total, in_pieces([lse, diag]), rest], axis=0).astype(out.dtype)


def join_body(tables, place, got_out, kept, got_q, cols, pair_out, q_grad, image_loss, text_loss):
    rows, caption = pair_out.shape[0], pair_out.shape[2]
    for row in range(rows):
        lines = slice(row * caption, (row + 1) * caption)
        for entry in range(NEGS):
            owner, _ = named(tables, 1, place[0] * rows + row, entry)
            block = got_out[owner].astype(F32)
            pair_out[row, entry] = block[lines].astype(BF16)
    total, lse, diag = add_lines([kept[...], got_q[...]], rows * caption)
    for row in range(rows):
        q_grad[row] = total[row * caption : (row + 1) * caption].astype(BF16)
    image_loss[...] = lse - diag
    n_cols = cols.shape[0]
    text_loss[...] = joined([cols[n, 0:1, :] for n in range(n_cols)]) - sum(
        cols[n, 1:2, :] for n in range(n_cols)
    )


def swap(part, axis, mask):
    return lax.ppermute(part, axis, [(s, s ^ mask) for s in range(lax.axis_size(axis))])


def gathered(block, axis):
    half = lax.axis_size(axis) // 2
    other = swap(block, axis, half)
    near = [block] + [swap(block, axis, mask) for mask in range(1, half)]
    far = [other] + [swap(other, axis, mask) for mask in range(1, half)]
    return near + far


def on_device(
    pictures,
    wordings,
    softness,
    queries,
    keys,
    values,
    img_owner,
    img_slot,
    txt_owner,
    txt_slot,
    img_cots,
    txt_cots,
):
    shape = jax.ShapeDtypeStruct
    vmem = pltpu.VMEM
    dma = lambda n: pltpu.SemaphoreType.DMA((n,))
    n_txt = lax.axis_size("txt")
    place = jnp.stack([lax.axis_index("txt"), lax.axis_index("img")]).astype(jnp.int32)
    local, caption, width = queries.shape
    patches = keys.shape[1]
    rows = padded(caption)
    everyone, half = n_txt * local, n_txt // 2
    block_shape = (n_txt, padded(local * caption + 1), width)
    wide_shape = (everyone + 1, rows, width)
    query_rows = -(-local * caption // 16) * 16
    held_shape = (n_txt, query_rows, width)
    pair_flops = 10 * caption * patches * width
    tables = jnp.concatenate([table.T for table in (img_owner, img_slot, txt_owner, txt_slot)], axis=0)
    sums = [vmem(keys.shape, F32), vmem(values.shape, F32)]
    lists = [pltpu.SMEM((local, everyone + 2 * CHUNK), jnp.int32), pltpu.SMEM((local,), jnp.int32)]

    step = fold_rows(pictures.shape, width)
    packed, both = kernel_call(
        pack_body,
        (shape((query_rows, width), BF16), shape((query_rows + step, width), BF16)),
        0,
        2,
        space=VMEM,
        mib=8,
    )(queries, pictures)
    other = swap(packed, "txt", half)
    near = [both] + [swap(both, "txt", mask) for mask in range(1, half)]
    parts = near + [other] + [swap(other, "txt", mask) for mask in range(1, half)]
    other_pictures = swap(pictures, "txt", half)
    far_pictures = [other_pictures] + [swap(other_pictures, "txt", mask) for mask in range(1, half)]
    after = (*parts[1:], *far_pictures)
    sent = kernel_call(
        send_body, shape(block_shape, BF16), 2, 1, space=VMEM, mib=12, n_after=len(after)
    )(tables, place, txt_cots, *after)
    got_cots = lax.all_to_all(sent, "txt", 0, 0, tiled=True)

    image_rows, n_texts, emb = pictures.shape[0], wordings.shape[0], wordings.shape[1]
    stats_shape = (n_txt, 1, 6 * image_rows)
    img_pair_out, image_terms, key_part, value_part, out = kernel_call(
        functools.partial(image_body, n_txt),
        (
            shape(img_cots.shape, BF16),
            shape(img_cots.shape, BF16),
            shape(keys.shape, F32),
            shape(values.shape, F32),
            shape(block_shape, BF16),
        ),
        2,
        n_txt + 3,
        [
            vmem(held_shape, BF16),
            vmem(wide_shape, F32),
            vmem(img_cots.shape, BF16),
            vmem((local * NEGS, rows, width), F32),
            vmem(keys.shape, BF16),
            vmem(values.shape, BF16),
            vmem(img_cots.shape, BF16),
            vmem(img_cots.shape, BF16),
            sums,
            vmem(wide_shape, F32),
            vmem(block_shape, BF16),
            *lists,
            dma(n_txt + 4),
        ],
        flops=6 * local * NEGS * pair_flops,
        nbytes=12_000_000,
    )(tables, place, *parts, img_cots, keys, values)
    got_out = lax.all_to_all(out, "txt", 0, 0, tiled=True)

    *q_out, key_grad, value_grad, col_stats = kernel_call(
        functools.partial(text_body, n_txt),
        [shape((2,) + block_shape[1:], BF16)] * half
        + [shape(keys.shape, BF16), shape(values.shape, BF16), shape((2, n_texts), F32)],
        3,
        n_txt + half + 7,
        [
            vmem(held_shape, BF16),
            vmem(wide_shape, F32),
            vmem(block_shape, BF16),
            vmem(wide_shape, F32),
            vmem(keys.shape, BF16),
            vmem(values.shape, BF16),
            vmem(img_cots.shape, BF16),
            vmem(wide_shape, F32),
            sums,
            sums,
            [vmem(keys.shape, BF16), vmem(values.shape, BF16)],
            vmem((half, step, width), BF16),
            vmem((n_txt,) + pictures.shape, BF16),
            vmem(wordings.shape, BF16),
            vmem((n_txt * image_rows, emb), BF16),
            vmem(wordings.shape, BF16),
            vmem(stats_shape, F32),
            vmem((2, n_texts), F32),
            *lists,
            dma(2 * n_txt + 4),
        ],
        flops=4 * local * NEGS * pair_flops,
        nbytes=10_000_000,
    )(
        tables, place, softness, *parts, *far_pictures, wordings, got_cots, keys, values,
        image_terms, key_part, value_part,
    )
    got_cols = lax.all_gather(tie(col_stats, q_out[0]), "img", axis=0)
    near = [q_out[0]] + [swap(block, "txt", 1 + n) for n, block in enumerate(q_out[1:])]
    kept, across = kernel_call(
        functools.partial(half_body, local * caption),
        (shape(block_shape[1:], F32), shape(block_shape[1:], BF16)),
        0,
        1 + half,
        space=VMEM,
        mib=12,
        nbytes=2_000_000,
    )(got_cols, *near)
    got_q = swap(across, "txt", half)

    txt_pair_out, query_grad, image_loss, text_loss = kernel_call(
        join_body,
        (
            shape(txt_cots.shape, BF16),
            shape(queries.shape, BF16),
            shape((1, image_rows), F32),
            shape((1, n_texts), F32),
        ),
        2,
        4,
        space=VMEM,
        mib=16,
    )(tables, place, got_out, kept, got_q, got_cols)
    return (
        image_loss.reshape(-1),
        text_loss.reshape(-1),
        img_pair_out,
        txt_pair_out,
        query_grad,
        key_grad,
        value_grad,
    )


def solution(mesh):
    every = ("img", "txt")
    three, four = P(every, None, None), P(every, None, None, None)
    table = P("img", None)
    return jax.shard_map(
        on_device,
        mesh=mesh,
        in_specs=(P(every, None), P("txt", None), P(), three, three, three)
        + (table, table, table, table, four, four),
        out_specs=(P(every), P("txt"), four, four, three, three, three),
        check_vma=False,
    )
```

```python
import functools

import jax
import jax.numpy as jnp
from jax import lax
from jax.experimental import pallas as pl
from jax.experimental.pallas import tpu as pltpu
from jax.sharding import PartitionSpec as P

NEGS = 4
EPSILON = 1e-06
LANES = 128
SMEM = pl.BlockSpec(memory_space=pltpu.SMEM)
ANY = pl.BlockSpec(memory_space=pl.ANY)
VMEM = pl.BlockSpec(memory_space=pltpu.VMEM)
F32 = jnp.float32
BF16 = jnp.bfloat16
NT = (((1,), (1,)), ((), ()))
TN = (((0,), (0,)), ((), ()))
NN = (((1,), (0,)), ((), ()))
CHUNK = 3


def kernel_call(body, out_shape, n_smem, n_any, scratch=(), flops=0, nbytes=0, space=ANY, mib=60, n_after=0, outs=None, **more):
    return pl.pallas_call(
        body,
        out_shape=out_shape,
        in_specs=[SMEM] * n_smem + [space] * n_any + [ANY] * n_after,
        out_specs=outs if outs is not None else jax.tree.map(lambda _: space, out_shape),
        scratch_shapes=list(scratch),
        compiler_params=pltpu.CompilerParams(vmem_limit_bytes=mib * 1024 * 1024),
        cost_estimate=pl.CostEstimate(flops=flops, bytes_accessed=nbytes, transcendentals=0),
        **more,
    )


def start_copies(pairs, sems, first=0):
    copies = [pltpu.make_async_copy(a, b, sems.at[first + n]) for n, (a, b) in enumerate(pairs)]
    for copy in copies:
        copy.start()
    return copies


def wait_copies(copies):
    for copy in copies:
        copy.wait()


def dot(a, b, dims):
    return lax.dot_general(a, b, dims, preferred_element_type=F32)


def padded(rows):
    return (rows + 7) // 8 * 8


def tie(value, *others):
    def body(*refs):
        del refs

    return kernel_call(
        body,
        jax.ShapeDtypeStruct(value.shape, value.dtype),
        0,
        1 + len(others),
        input_output_aliases={0: 0},
    )(value, *others)


def pack_body(queries, packed):
    captions, caption = queries.shape[:2]
    pieces = [queries[row].astype(F32) for row in range(captions)]
    pieces.append(jnp.zeros((packed.shape[0] - captions * caption, packed.shape[1]), F32))
    packed[...] = jnp.concatenate(pieces, axis=0).astype(BF16)


def both_body(packed, pictures, both, again):
    first, emb = packed.shape[0], pictures.shape[1]
    both[0:first, :] = packed[...]
    both[first:, :] = jnp.zeros((both.shape[0] - first, packed.shape[1]), BF16)
    for fold, (start, count) in enumerate(folds(pictures.shape, packed.shape[1])):
        both[first : first + count, fold * emb : (fold + 1) * emb] = pictures[start : start + count]
    again[...] = pictures[...]


def fold_rows(shape, width):
    return -(-shape[0] // (width // shape[1] * 16)) * 16


def folds(shape, width):
    step = fold_rows(shape, width)
    return [(start, min(step, shape[0] - start)) for start in range(0, shape[0], step)]


def named(tables, of_captions, row, entry):
    first = 2 * NEGS * of_captions
    return tables[first + entry, row], tables[first + NEGS + entry, row]


def send_body(tables, place, cots, sent, blocks, sems):
    rows, caption = cots.shape[0], cots.shape[2]
    copies = []
    for part in range(blocks.shape[0]):
        pieces = []
        for row in range(rows):
            at = jnp.int32(0)
            for entry in range(NEGS):
                owner, _ = named(tables, 1, place[0] * rows + row, entry)
                at = jnp.where(owner == part, entry, at)
            pieces.append(cots[row, at].astype(F32))
        pieces.append(jnp.zeros((blocks.shape[1] - rows * caption, blocks.shape[2]), F32))
        blocks[part] = jnp.concatenate(pieces, axis=0).astype(BF16)
        copies += start_copies([(blocks.at[part], sent.at[part])], sems, part)
    wait_copies(copies)


def in_pieces(values):
    pieces = []
    for value in values:
        for _ in range(3):
            pieces.append(value.astype(BF16).astype(F32))
            value = value - pieces[-1]
    return jnp.concatenate(pieces, axis=1)


def from_pieces(line):
    width = line.shape[1] // 6
    pieces = [line[:, n * width : (n + 1) * width] for n in range(6)]
    return pieces[0] + pieces[1] + pieces[2], pieces[3] + pieces[4] + pieces[5]


def joined(parts):
    highest = functools.reduce(jnp.maximum, parts)
    return highest + jnp.log(sum(jnp.exp(part - highest) for part in parts))


def contrast(n_parts, place, softness, near_in, images_in, texts_in, unit_images, unit_texts, row_stats, col_stats):
    rows, emb = images_in.shape[1:]

    def unit(source):
        wide = source.astype(F32)
        factor = lax.rsqrt(jnp.sum(wide * wide, axis=-1, keepdims=True) + EPSILON)
        return (wide * factor).astype(BF16)

    unit_texts[...] = unit(texts_in[...])
    for part in range(n_parts // 2):
        for fold, (start, count) in enumerate(folds((rows, emb), near_in.shape[2])):
            images_in[part, start : start + count, :] = near_in[part, 0:count, fold * emb : (fold + 1) * emb]
    for part in range(n_parts):
        first = jnp.bitwise_xor(part, place[0]) * rows
        unit_images[pl.ds(pl.multiple_of(first, 16), rows), :] = unit(images_in[part])
    undo = 1.0 / softness[0]
    n_images, n_texts = n_parts * rows, texts_in.shape[0]
    first_image, first_text = place[1] * n_images, place[0] * n_texts

    def stats(long, long_first, short, short_first, count):
        blocks = range(0, short.shape[0], count)
        logits = [dot(long[...], short[at : at + count, :], NT) * undo for at in blocks]
        highest = [jnp.max(block, axis=0, keepdims=True) for block in logits]
        total = [
            jnp.sum(jnp.exp(block - top), axis=0, keepdims=True) for block, top in zip(logits, highest)
        ]
        for at, block, top, whole in zip(blocks, logits, highest, total):
            on_diag = (lax.broadcasted_iota(jnp.int32, block.shape, 0) + long_first) == (
                lax.broadcasted_iota(jnp.int32, block.shape, 1) + (short_first + at)
            )
            diag = jnp.sum(jnp.where(on_diag, block, 0.0), axis=0, keepdims=True)
            yield at, (top + jnp.log(whole), diag)

    for at, found in stats(unit_texts, first_text, unit_images, first_image, rows):
        row_stats[at // rows] = in_pieces(found)
    for at, found in stats(unit_images, first_image, unit_texts, first_text, LANES):
        for n, value in enumerate(found):
            col_stats[n : n + 1, at : at + LANES] = value


def attend(chunks, queries, cots, keys, values, sums):
    half = LANES // 2
    tiles = [slice(n * LANES, (n + 1) * LANES) for n in range(keys.shape[2] // LANES)]
    work = [(chunk, lanes) for chunk in chunks for lanes in tiles]

    def stacked(ref, at, lanes):
        pieces = [ref[n, :, lanes] for n in at]
        pieces.append(jnp.zeros((LANES - len(at) * ref.shape[1], LANES), F32))
        tile = jnp.concatenate(pieces, axis=0)
        low = lax.broadcasted_iota(jnp.int32, tile.shape, 1) < half
        pair = jnp.concatenate([jnp.where(low, tile, 0.0), jnp.where(low, 0.0, tile)], axis=0)
        return pair.astype(BF16)

    def folded(pair):
        return jnp.transpose(jnp.concatenate([pair[:half, :LANES], pair[half:, LANES:]], axis=0))

    q = [stacked(queries, chunk[1], lanes) for chunk, lanes in work]
    logits = [dot(keys[chunk[0], :, lanes], q[n], NT) for n, (chunk, lanes) in enumerate(work)]
    if cots is not None:
        g = [stacked(cots, chunk[2], lanes) for chunk, lanes in work]
        terms = [dot(values[chunk[0], :, lanes], g[n], NT) for n, (chunk, lanes) in enumerate(work)]
    weights = []
    for logit in logits:
        shifted = jnp.exp(logit - jnp.max(logit, axis=0, keepdims=True))
        weights.append(shifted * (1.0 / jnp.sum(shifted, axis=0, keepdims=True)))
    rounded = [weight.astype(BF16) for weight in weights]
    outputs = [
        dot(values[chunk[0], :, lanes], rounded[n], TN) if chunk[3] is not None else None
        for n, (chunk, lanes) in enumerate(work)
    ]
    if cots is not None:
        key_sum, value_sum = sums
        value_terms = [dot(rounded[n], g[n], NN) for n in range(len(work))]
        logit_terms = []
        for weight, term in zip(weights, terms):
            inner = jnp.sum(weight * term, axis=0, keepdims=True)
            logit_terms.append((weight * (term - inner)).astype(BF16))
        q_terms = [dot(keys[chunk[0], :, lanes], logit_terms[n], TN) for n, (chunk, lanes) in enumerate(work)]
        key_terms = [dot(logit_terms[n], q[n], NN) for n in range(len(work))]
        for n, (chunk, lanes) in enumerate(work):
            key_sum[chunk[0], :, lanes] += key_terms[n]
            value_sum[chunk[0], :, lanes] += value_terms[n]
    for n, (chunk, lanes) in enumerate(work):
        if chunk[3] is not None:
            chunk[3](lanes, folded(outputs[n]))
        if chunk[4] is not None:
            chunk[4](lanes, folded(q_terms[n]) * 0.125)


def widen(source, wide, at, scale=1.0):
    caption = source.shape[0]
    wide[at, caption:, :] = jnp.zeros((wide.shape[1] - caption, wide.shape[2]), F32)
    wide[at, 0:caption, :] = source.astype(F32) * scale


def query_copies(parts, held):
    lines = pl.ds(0, held.shape[1])
    return [(part.at[lines], held.at[n]) for n, part in enumerate(parts)]


def widen_block(block, wide, first, captions, caption):
    for row in range(captions):
        wide[first + row, caption:, :] = jnp.zeros((wide.shape[1] - caption, wide.shape[2]), F32)
        wide[first + row, 0:caption, :] = block[row * caption : (row + 1) * caption]


def widen_queries(held, queries, captions, caption):
    n_parts = held.shape[0]
    for part in range(n_parts):
        widen_block(held[part].astype(F32) * 0.125, queries, part * captions, captions, caption)
    if queries.shape[0] > n_parts * captions:
        queries[n_parts * captions] = jnp.zeros(queries.shape[1:], F32)


def find_listed(tables, place, lists, counts, everyone):
    for image in range(counts.shape[0]):
        counts[image] = 0

        def clear(i, _, image=image):
            lists[image, i] = everyone
            return 0

        lax.fori_loop(0, lists.shape[1], clear, 0)

    def find(j, _):
        for entry in range(NEGS):
            owner, image = named(tables, 1, j, entry)

            @pl.when(owner == place[0])
            def _():
                lists[image, counts[image]] = j
                counts[image] = counts[image] + 1

        return 0

    lax.fori_loop(0, everyone, find, 0)


def each_pair_of_chunks(lists, counts, place, captions, everyone, work):
    images = counts.shape[0]
    needed = [(counts[image] + CHUNK - 1) // CHUNK for image in range(images)]

    def pair_step(pair, _):
        chunks = []
        for n in range(2):
            chunk = 2 * pair + n
            image, first, past = jnp.int32(0), jnp.int32(0), jnp.int32(0)
            for later in range(1, images):
                past = past + needed[later - 1]
                image = jnp.where(chunk >= past, later, image)
                first = jnp.where(chunk >= past, past, first)
            j = [lists[image, (chunk - first) * CHUNK + e] for e in range(CHUNK)]
            q_at = [
                jnp.where(
                    n < everyone,
                    jnp.bitwise_xor(n // captions, place[0]) * captions + n % captions,
                    everyone,
                )
                for n in j
            ]
            chunks.append((image, j, q_at))
        work(chunks)
        return 0

    lax.fori_loop(0, (sum(needed) + 1) // 2, pair_step, 0)


def image_body(n_parts, tables, place, softness, *refs):
    half = n_parts // 2
    parts, pictures, refs = refs[:n_parts], refs[n_parts : n_parts + half], refs[n_parts + half :]
    (texts, cots_in, keys_in, values_in, image_out, image_terms, key_out, value_out, text_out, row_out, col_out,
     held, queries, cots_held, cots, keys, values, image_outs, terms, sums, outs, blocks,
     near_in, images_in, texts_in, unit_images, unit_texts, row_stats, col_stats, lists, counts, sems) = refs
    images = captions = keys.shape[0]
    caption = cots_held.shape[2]
    rows = queries.shape[1]
    everyone = n_parts * captions
    soon = start_copies(
        [(texts, texts_in)]
        + [(part.at[pl.ds(held.shape[1], near_in.shape[1])], near_in.at[n]) for n, part in enumerate(parts[:half])]
        + [(picture, images_in.at[half + n]) for n, picture in enumerate(pictures)],
        sems,
    )
    copies = start_copies(
        query_copies(parts, held) + [(cots_in, cots_held), (keys_in, keys), (values_in, values)],
        sems,
        len(soon),
    )
    find_listed(tables, place, lists, counts, everyone)
    for total in (*sums, outs):
        total[...] = jnp.zeros_like(total)
    wait_copies(soon)
    contrast(
        n_parts, place, softness, near_in, images_in, texts_in, unit_images, unit_texts, row_stats, col_stats
    )
    wait_copies(copies)
    widen_queries(held, queries, captions, caption)
    for image in range(images):
        for entry in range(NEGS):
            widen(cots_held[image, entry], cots, image * NEGS + entry)
    for first in range(0, NEGS, CHUNK):
        entries = range(first, min(first + CHUNK, NEGS))
        chunks = []
        for image in range(images):
            at = []
            for entry in entries:
                owner, slot = named(tables, 0, place[0] * images + image, entry)
                at.append(jnp.bitwise_xor(owner, place[0]) * captions + slot)

            def emit(ref, lanes, value, image=image, entries=entries):
                for n, e in enumerate(entries):
                    ref[image, e, :, lanes] = value[n * rows : n * rows + caption].astype(BF16)

            chunks.append(
                (
                    image, at, [image * NEGS + e for e in entries],
                    functools.partial(emit, image_outs), functools.partial(emit, terms),
                )
            )
        attend(chunks, queries, cots, keys, values, sums)
    copies = start_copies(
        [(image_outs, image_out), (terms, image_terms), *zip(sums, (key_out, value_out))]
        + [(row_stats, row_out), (col_stats, col_out)],
        sems,
    )

    def work(chunks):
        def emit_out(j, lanes, output):
            for e in range(CHUNK):
                outs[j[e], :, lanes] = output[e * rows : (e + 1) * rows]

        attend(
            [
                (image, q_at, None, functools.partial(emit_out, j), None)
                for image, j, q_at in chunks
            ],
            queries, None, keys, values, None,
        )

    each_pair_of_chunks(lists, counts, place, captions, everyone, work)
    for part in range(n_parts):
        pieces = [outs[part * captions + row, 0:caption, :] for row in range(captions)]
        pieces.append(jnp.zeros((blocks.shape[1] - captions * caption, blocks.shape[2]), F32))
        blocks[part] = jnp.concatenate(pieces, axis=0).astype(BF16)
        copies += start_copies([(blocks.at[part], text_out.at[part])], sems, 6 + part)
    wait_copies(copies)


def text_body(n_parts, tables, place, *refs):
    half = n_parts // 2
    parts, refs = refs[:n_parts], refs[n_parts:]
    (cots_in, keys_in, values_in, stats_in, terms_in, key_in, value_in), refs = refs[:7], refs[7:]
    q_out, refs = refs[:half], refs[half:]
    (key_grad, value_grad,
     held, queries, cots_held, cots, keys, values, row_stats, terms, q_sum, firsts, sums, grads,
     lists, counts, sems) = refs
    images = captions = keys.shape[0]
    caption = terms.shape[2]
    rows = queries.shape[1]
    everyone = n_parts * captions
    copies = start_copies(
        query_copies(parts, held) + [(cots_in, cots_held), (keys_in, keys), (values_in, values)],
        sems,
    )
    find_listed(tables, place, lists, counts, everyone)
    for total in (*sums, q_sum):
        total[...] = jnp.zeros_like(total)
    wait_copies(copies)
    later = start_copies(
        [(stats_in, row_stats), (terms_in, terms), *zip((key_in, value_in), firsts)], sems
    )
    out = []
    widen_queries(held, queries, captions, caption)
    for part in range(n_parts):
        widen_block(cots_held[part].astype(F32), cots, part * captions, captions, caption)
    cots[everyone] = jnp.zeros(cots.shape[1:], F32)

    def work(chunks):
        def emit_q(q_at, lanes, term):
            for e in range(CHUNK):
                q_sum[q_at[e], :, lanes] += term[e * rows : (e + 1) * rows].astype(BF16).astype(F32)

        attend(
            [(image, q_at, j, None, functools.partial(emit_q, q_at)) for image, j, q_at in chunks],
            queries, cots, keys, values, sums,
        )

    each_pair_of_chunks(lists, counts, place, captions, everyone, work)
    wait_copies(later)
    for image in range(images):
        for entry in range(NEGS):
            owner, slot = named(tables, 0, place[0] * images + image, entry)
            at = jnp.bitwise_xor(owner, place[0]) * captions + slot
            q_sum[at, 0:caption, :] += terms[image, entry].astype(F32)
    block_rows = cots_held.shape[1]
    for part in range(n_parts):
        target = jnp.bitwise_xor(part, place[0])
        pieces = [q_sum[part * captions + row, 0:caption, :] for row in range(captions)]
        pieces.append(row_stats[target])
        pieces.append(jnp.zeros((block_rows - captions * caption - 1, cots_held.shape[2]), F32))
        cots_held[part] = jnp.concatenate(pieces, axis=0).astype(BF16)
        out += start_copies([(cots_held.at[part], q_out[part % half].at[part // half])], sems, part)
    for n, grad in enumerate((key_grad, value_grad)):
        for image in range(images):
            grads[n][image] = (sums[n][image] + firsts[n][image]).astype(BF16)
        out += start_copies([(grads[n], grad)], sems, n_parts + n)
    wait_copies(out)


def add_lines(blocks, lines):
    total = blocks[0].astype(F32)
    for block in blocks[1:]:
        total = total + block.astype(F32)
    found = [from_pieces(block[lines : lines + 1].astype(F32)) for block in blocks]
    return total[0:lines], joined([lse for lse, _ in found]), sum(diag for _, diag in found)


def half_body(lines, after, *refs):
    del after
    blocks, kept, sent = refs[:-2], refs[-2], refs[-1]
    for side, out in enumerate((kept, sent)):
        total, lse, diag = add_lines([block[side] for block in blocks], lines)
        rest = jnp.zeros((out.shape[0] - lines - 1, out.shape[1]), F32)
        out[...] = jnp.concatenate([total, in_pieces([lse, diag]), rest], axis=0).astype(out.dtype)


def pair_out_body(tables, place, got_out, pair_out):
    rows, caption = pair_out.shape[0], pair_out.shape[2]
    for row in range(rows):
        lines = slice(row * caption, (row + 1) * caption)
        for entry in range(NEGS):
            owner, _ = named(tables, 1, place[0] * rows + row, entry)
            block = got_out[owner].astype(F32)
            pair_out[row, entry] = block[lines].astype(BF16)


def join_body(kept, got_q, cols, q_grad, image_loss, text_loss):
    rows, caption = q_grad.shape[:2]
    total, lse, diag = add_lines([kept[...], got_q[...]], rows * caption)
    for row in range(rows):
        q_grad[row] = total[row * caption : (row + 1) * caption].astype(BF16)
    image_loss[...] = lse - diag
    n_cols = cols.shape[0]
    text_loss[...] = joined([cols[n, 0:1, :] for n in range(n_cols)]) - sum(
        cols[n, 1:2, :] for n in range(n_cols)
    )


def swap(part, axis, mask):
    return lax.ppermute(part, axis, [(s, s ^ mask) for s in range(lax.axis_size(axis))])


def gathered(block, axis):
    half = lax.axis_size(axis) // 2
    other = swap(block, axis, half)
    near = [block] + [swap(block, axis, mask) for mask in range(1, half)]
    far = [other] + [swap(other, axis, mask) for mask in range(1, half)]
    return near + far


def on_device(
    pictures,
    wordings,
    softness,
    queries,
    keys,
    values,
    img_owner,
    img_slot,
    txt_owner,
    txt_slot,
    img_cots,
    txt_cots,
):
    shape = jax.ShapeDtypeStruct
    vmem = pltpu.VMEM
    dma = lambda n: pltpu.SemaphoreType.DMA((n,))
    n_txt = lax.axis_size("txt")
    place = jnp.stack([lax.axis_index("txt"), lax.axis_index("img")]).astype(jnp.int32)
    local, caption, width = queries.shape
    patches = keys.shape[1]
    rows = padded(caption)
    everyone, half = n_txt * local, n_txt // 2
    block_shape = (n_txt, padded(local * caption + 1), width)
    wide_shape = (everyone + 1, rows, width)
    query_rows = -(-local * caption // 16) * 16
    held_shape = (n_txt, query_rows, width)
    pair_flops = 10 * caption * patches * width
    tables = jnp.concatenate([table.T for table in (img_owner, img_slot, txt_owner, txt_slot)], axis=0)
    sums = [vmem(keys.shape, F32), vmem(values.shape, F32)]
    lists = [pltpu.SMEM((local, everyone + 2 * CHUNK), jnp.int32), pltpu.SMEM((local,), jnp.int32)]

    step = fold_rows(pictures.shape, width)
    packed = kernel_call(pack_body, shape((query_rows, width), BF16), 0, 1, space=VMEM, mib=8)(queries)
    both, again = kernel_call(
        both_body,
        (shape((query_rows + step, width), BF16), shape(pictures.shape, BF16)),
        0,
        2,
        space=VMEM,
        mib=8,
    )(packed, pictures)
    other = swap(packed, "txt", half)
    near = [both] + [swap(both, "txt", mask) for mask in range(1, half)]
    parts = near + [other] + [swap(other, "txt", mask) for mask in range(1, half)]
    other_pictures = swap(again, "txt", half)
    far_pictures = [other_pictures] + [swap(other_pictures, "txt", mask) for mask in range(1, half)]
    sent = kernel_call(
        send_body,
        shape(block_shape, BF16),
        2,
        1,
        [vmem(block_shape, BF16), dma(n_txt)],
        space=VMEM,
        mib=12,
        outs=ANY,
    )(tables, place, txt_cots)
    ready = tie(sent, *parts[1:], *far_pictures, keys, values, img_cots)
    got_cots = lax.all_to_all(ready, "txt", 0, 0, tiled=True)

    image_rows, n_texts, emb = pictures.shape[0], wordings.shape[0], wordings.shape[1]
    stats_shape = (n_txt, 1, 6 * image_rows)
    img_pair_out, image_terms, key_part, value_part, out, row_stats, col_stats = kernel_call(
        functools.partial(image_body, n_txt),
        (
            shape(img_cots.shape, BF16),
            shape(img_cots.shape, BF16),
            shape(keys.shape, F32),
            shape(values.shape, F32),
            shape(block_shape, BF16),
            shape(stats_shape, F32),
            shape((2, n_texts), F32),
        ),
        3,
        n_txt + half + 4,
        [
            vmem(held_shape, BF16),
            vmem(wide_shape, F32),
            vmem(img_cots.shape, BF16),
            vmem((local * NEGS, rows, width), F32),
            vmem(keys.shape, BF16),
            vmem(values.shape, BF16),
            vmem(img_cots.shape, BF16),
            vmem(img_cots.shape, BF16),
            sums,
            vmem(wide_shape, F32),
            vmem(block_shape, BF16),
            vmem((half, step, width), BF16),
            vmem((n_txt,) + pictures.shape, BF16),
            vmem(wordings.shape, BF16),
            vmem((n_txt * image_rows, emb), BF16),
            vmem(wordings.shape, BF16),
            vmem(stats_shape, F32),
            vmem((2, n_texts), F32),
            *lists,
            dma(2 * n_txt + 6),
        ],
        flops=6 * local * NEGS * pair_flops,
        nbytes=12_000_000,
    )(tables, place, softness, *parts, *far_pictures, wordings, img_cots, keys, values)
    got_out = lax.all_to_all(out, "txt", 0, 0, tiled=True)

    *q_out, key_grad, value_grad = kernel_call(
        functools.partial(text_body, n_txt),
        [shape((2,) + block_shape[1:], BF16)] * half
        + [shape(keys.shape, BF16), shape(values.shape, BF16)],
        2,
        n_txt + 7,
        [
            vmem(held_shape, BF16),
            vmem(wide_shape, F32),
            vmem(block_shape, BF16),
            vmem(wide_shape, F32),
            vmem(keys.shape, BF16),
            vmem(values.shape, BF16),
            vmem(stats_shape, F32),
            vmem(img_cots.shape, BF16),
            vmem(wide_shape, F32),
            sums,
            sums,
            [vmem(keys.shape, BF16), vmem(values.shape, BF16)],
            *lists,
            dma(2 * n_txt + 4),
        ],
        flops=4 * local * NEGS * pair_flops,
        nbytes=10_000_000,
    )(
        tables, place, *parts, got_cots, keys, values, row_stats, image_terms, key_part, value_part
    )
    got_cols = lax.all_gather(tie(col_stats, q_out[0]), "img", axis=0)
    near = [q_out[0]] + [swap(block, "txt", 1 + n) for n, block in enumerate(q_out[1:])]
    kept, across = kernel_call(
        functools.partial(half_body, local * caption),
        (shape(block_shape[1:], F32), shape(block_shape[1:], BF16)),
        0,
        1 + half,
        space=VMEM,
        mib=12,
        nbytes=2_000_000,
    )(got_cols, *near)
    got_q = swap(across, "txt", half)

    txt_pair_out = kernel_call(
        pair_out_body, shape(txt_cots.shape, BF16), 2, 1, space=VMEM, mib=12, nbytes=2_000_000
    )(tables, place, got_out)
    query_grad, image_loss, text_loss = kernel_call(
        join_body,
        (shape(queries.shape, BF16), shape((1, image_rows), F32), shape((1, n_texts), F32)),
        0,
        3,
        space=VMEM,
        mib=12,
        nbytes=1_000_000,
    )(kept, got_q, got_cols)
    return (
        image_loss.reshape(-1),
        text_loss.reshape(-1),
        img_pair_out,
        txt_pair_out,
        query_grad,
        key_grad,
        value_grad,
    )


def solution(mesh):
    every = ("img", "txt")
    three, four = P(every, None, None), P(every, None, None, None)
    table = P("img", None)
    return jax.shard_map(
        on_device,
        mesh=mesh,
        in_specs=(P(every, None), P("txt", None), P(), three, three, three)
        + (table, table, table, table, four, four),
        out_specs=(P(every), P("txt"), four, four, three, three, three),
        check_vma=False,
    )
```
